32 devices in a mesh: seq: 16 (over z, y, core), head: 2 (over x).
Axes of the slice: x: 2, y: 2, z: 4, core: 2. Of those that a mesh axis runs over, the one named last changes fastest.
Arguments:
- query_rows: bfloat16 [5120, 3072], P('seq', 'head'), may hold values from -6 to 6
- key_rows: bfloat16 [5120, 3072], P('seq', 'head'), may hold values from -6 to 6
- value_rows: bfloat16 [5120, 3072], P('seq', 'head'), may hold values from -6 to 6
- pattern: int32 [16, 6], P('seq'), may hold values 0 or 1
- owners: int32 [4], replicated, may hold values from 0 to 15, as said below
- out_weight: bfloat16 [3072, 3072], P('head'), may hold values from -0.15625 to 0.15625
Outputs:
- mixed: bfloat16 [5120, 3072], P('seq', 'head')
The draws below stay inside these ranges and needn't reach their ends.
Inputs may be any that keep to these rules, and one draw needn't show every extreme that they name: `owners`: distinct block indices; blocks 0 and 16 - 1 are always among them.
All inputs are finite; a program needn't handle non-finite values. No bound on the sum of `pattern` on one device may be relied on, other than what follows from the above.
Results may differ from the reference program's by a relative error of at most 0.02.
Values may be sent and summed in bfloat16 or wider, within the bound.
No kernel may reach another device: no remote copies, remote signals or barrier semaphores. Data moves between devices by JAX's collectives and lax.ppermute only.
A program may use at most 128 MiB of HBM per device.

```python
import jax
import jax.numpy as jnp
from jax import lax

D = 3072
HEADS = 24
HD = 128
TOK_DEV = 320
REACH = 3
OWNERS = 4
REFS = 1024
REF_DEV = 256
TOKENS = 5120
N_SEQ = 16
N_HEAD = 2


def shared_pair(key):
    first = jax.random.fold_in(key, 11)
    second = jax.random.fold_in(key, 23)
    width = HEADS * HD
    queries = jnp.clip(jax.random.normal(first, (TOKENS, width), jnp.float32), -6.0, 6.0)
    keys_all = jnp.clip(jax.random.normal(second, (TOKENS, width), jnp.float32), -6.0, 6.0)
    return (queries, keys_all)


def draw_query_rows(key, part):
    return shared_pair(key)[0].astype(jnp.bfloat16)


def draw_key_rows(key, part):
    return shared_pair(key)[1].astype(jnp.bfloat16)


def draw_owners(key, part):
    inner = jax.random.permutation(jax.random.fold_in(key, 5), N_SEQ - 2) + 1
    picked = jnp.concatenate([jnp.array([0, N_SEQ - 1], dtype=jnp.int32), inner[:OWNERS - 2].astype(jnp.int32)])
    return jax.random.permutation(jax.random.fold_in(key, 7), picked).astype(jnp.int32)


def place_ends(result, rng, smallest, top_value):
    longest = result.shape.index(max(result.shape))
    spots = []
    for shift in (0, 1):
        where = [jax.random.randint(jax.random.fold_in(rng, axis), (), 0, length) for axis, length in enumerate(result.shape)]
        where[longest] = (where[longest] + shift) % result.shape[longest]
        spots.append(tuple(where))
    return result.at[spots[0]].set(smallest).at[spots[1]].set(top_value)


def with_spikes(result, key, source, target, parts, factor):
    def block_of(position):
        return (jnp.arange(result.shape[position]) // (result.shape[position] // parts)).reshape((-1,) + (1,) * (result.ndim - 1 - position))

    first = jax.random.permutation(key, parts)[block_of(target)]
    second = (block_of(target) + parts // 2) % parts
    return jnp.where((block_of(source) == first) | (block_of(source) == second), factor * result, result)


def levels(rng, extent, cuts, low, top_value):
    def one(axis_at, shards_of):
        draws = jax.random.uniform(jax.random.fold_in(jax.random.fold_in(rng, 6), axis_at), (shards_of,), jnp.float32, low / len(cuts), top_value / len(cuts))
        return jnp.repeat(jnp.exp(draws), extent[axis_at] // shards_of).reshape((-1,) + (1,) * (len(extent) - axis_at - 1))

    gain = one(*cuts[0])
    for cut in cuts[1:]:
        gain = gain * one(*cut)
    return gain


def centred(key, dims, scale, most, pieces=(), kind=jnp.bfloat16):
    result = scale * jax.random.normal(key, dims, jnp.float32)
    if pieces:
        result = result * levels(key, dims, pieces, -0.22, 0.18)
    return jnp.clip(result, -most, most).astype(kind)


def gaussian_with(key, shape, scale, limit, pieces, heavy, kind=jnp.bfloat16):
    result = scale * jax.random.normal(key, shape, jnp.float32)
    if pieces:
        result = result * levels(key, shape, pieces, -0.22, 0.18)
    return jnp.clip(with_spikes(result, jax.random.fold_in(key, 3), *heavy), -limit, limit).astype(kind)


def setup_inputs(seed: int = 0) -> dict:
    key_of = jax.random.split(jax.random.key(seed), 7)
    return {
        "query_rows": draw_query_rows(jax.random.fold_in(key_of[6], 71), 0),
        "key_rows": draw_key_rows(jax.random.fold_in(key_of[6], 71), 0),
        "value_rows": centred(key_of[2], (TOKENS, HEADS * HD), 1.0, 6.0, ((0, 16), (1, 2))),
        "pattern": place_ends((jax.random.randint(key_of[3], (N_SEQ, 2 * REACH), 0, 3) < 1).astype(jnp.int32), jax.random.fold_in(key_of[3], 1), 0, 1),
        "owners": draw_owners(jax.random.fold_in(key_of[6], 71), 0),
        "out_weight": gaussian_with(key_of[5], (HEADS * HD, D), (HEADS * HD) ** -0.5, 0.15625, ((0, 2),), (0, 1, 2, 2.0)),
    }


def column_of(offset):
    return offset + REACH if offset < 0 else offset + REACH - 1


def reference(query_rows, key_rows, value_rows, pattern, owners, out_weight):
    scale = HD ** -0.5
    ref_keys = jnp.concatenate([lax.dynamic_slice_in_dim(key_rows, (owners[member] * TOK_DEV).astype(jnp.int32), REF_DEV, 0) for member in range(OWNERS)], axis=0)
    ref_values = jnp.concatenate([lax.dynamic_slice_in_dim(value_rows, (owners[member] * TOK_DEV).astype(jnp.int32), REF_DEV, 0) for member in range(OWNERS)], axis=0)

    def one_block(block):
        block = block.astype(jnp.int32)
        queries = lax.dynamic_slice_in_dim(query_rows, block * TOK_DEV, TOK_DEV, 0)
        key_list = []
        value_list = []
        mask_list = []
        for offset in range(-REACH, REACH + 1):
            source = ((block + offset) % N_SEQ).astype(jnp.int32)
            key_list.append(lax.dynamic_slice_in_dim(key_rows, source * TOK_DEV, TOK_DEV, 0))
            value_list.append(lax.dynamic_slice_in_dim(value_rows, source * TOK_DEV, TOK_DEV, 0))
            if offset == 0:
                active = jnp.ones((), dtype=bool)
            else:
                active = pattern[block, column_of(offset)] != 0
            mask_list.append(jnp.broadcast_to(active, (TOK_DEV,)))
        key_list.append(ref_keys)
        value_list.append(ref_values)
        mask_list.append(jnp.ones((REFS,), dtype=bool))
        all_keys = jnp.concatenate(key_list, axis=0).astype(jnp.float32).reshape(-1, HEADS, HD)
        all_values = jnp.concatenate(value_list, axis=0).astype(jnp.float32).reshape(-1, HEADS, HD)
        key_mask = jnp.concatenate(mask_list, axis=0)
        query_three = queries.astype(jnp.float32).reshape(TOK_DEV, HEADS, HD)
        scores = jnp.einsum('qhd,khd->hqk', query_three, all_keys) * scale
        scores = jnp.where(key_mask[None, None, :], scores, -jnp.inf)
        peaks = jnp.max(scores, axis=-1, keepdims=True)
        weights = jnp.exp(scores - peaks)
        totals = jnp.sum(weights, axis=-1)
        rounded = weights.astype(jnp.bfloat16).astype(jnp.float32)
        summed = jnp.einsum('hqk,khd->hqd', rounded, all_values)
        attended = summed / totals[:, :, None]
        return jnp.transpose(attended, (1, 0, 2)).reshape(TOK_DEV, HEADS * HD).astype(jnp.bfloat16)

    attended = lax.map(one_block, jnp.arange(N_SEQ, dtype=jnp.int32))
    attended = attended.reshape(TOKENS, HEADS * HD)
    group_width = HEADS * HD // N_HEAD
    mixed = jnp.zeros((TOKENS, D), jnp.float32)
    for group in range(N_HEAD):
        partial_value = jnp.dot(attended[:, group * group_width:(group + 1) * group_width], out_weight[group * group_width:(group + 1) * group_width], preferred_element_type=jnp.float32)
        mixed = mixed + partial_value.astype(jnp.bfloat16).astype(jnp.float32)
    return mixed.astype(jnp.bfloat16)
```

```python
import functools

import jax
import jax.numpy as jnp
from jax import lax
from jax.experimental import pallas as pl
from jax.experimental.pallas import tpu as pltpu
from jax.sharding import PartitionSpec as P

HD = 128
REACH = 3
OWNERS = 4
REF_DEV = 256
GROUP = 4
PLANES = 4
CHUNKS = (2, 1)
PAT_ROWS = 16
NEG = -1e30
LOG2E = 1.4426950408889634
F32 = jnp.float32
BF16 = jnp.bfloat16


def broadcast(block, axis, owner):
    block = jnp.where(lax.axis_index(axis) == owner, block, jnp.zeros_like(block))
    return lax.psum(block, axis)


def from_behind(value, axis, steps):
    count = lax.axis_size(axis)
    pairs = [(source, (source + steps) % count) for source in range(count)]
    return lax.ppermute(value, axis, pairs)


def column_of(offset):
    return offset + REACH if offset < 0 else offset + REACH - 1


def merge_block(state, query_three, block_keys, block_values):
    peaks, totals, summed_values = state
    local_heads = query_three.shape[1]
    keys_three = block_keys.reshape(-1, local_heads, HD)
    values_three = block_values.reshape(-1, local_heads, HD)
    scores = jnp.einsum(
        "qhd,khd->hqk", query_three, keys_three, preferred_element_type=jnp.float32
    ) * HD ** (-0.5)
    new_peaks = jnp.maximum(peaks, jnp.max(scores, axis=-1))
    rescale = jnp.exp(peaks - new_peaks)
    weights = jnp.exp(scores - new_peaks[:, :, None])
    totals = totals * rescale + jnp.sum(weights, axis=-1)
    contrib = jnp.einsum(
        "hqk,khd->hqd",
        weights.astype(jnp.bfloat16),
        values_three,
        preferred_element_type=jnp.float32,
    )
    summed_values = summed_values * rescale[:, :, None] + contrib
    return (new_peaks, totals, summed_values)


def absorb(state, query_three, stacked, active):
    return lax.cond(
        active,
        lambda inner: merge_block(inner, query_three, stacked[0], stacked[1]),
        lambda inner: inner,
        state,
    )


def plain_body(query_rows, key_rows, value_rows, pattern, owners, out_weight):
    row_count = query_rows.shape[0]
    local_width = query_rows.shape[1]
    local_heads = local_width // HD
    query_three = query_rows.reshape(row_count, local_heads, HD)
    start_state = (
        jnp.full((local_heads, row_count), -jnp.inf, jnp.float32),
        jnp.zeros((local_heads, row_count), jnp.float32),
        jnp.zeros((local_heads, row_count, HD), jnp.float32),
    )
    state = merge_block(start_state, query_three, key_rows, value_rows)
    own_stack = jnp.stack([key_rows, value_rows])
    ref_stack = jnp.stack([key_rows[:REF_DEV], value_rows[:REF_DEV]])
    for member in range(OWNERS):
        arrived = broadcast(ref_stack, "seq", owners[member])
        state = merge_block(state, query_three, arrived[0], arrived[1])
    for distance in range(1, REACH + 1):
        for offset in (-distance, distance):
            arrived = from_behind(own_stack, "seq", -offset)
            state = absorb(state, query_three, arrived, pattern[0, column_of(offset)] != 0)
    peaks, totals, summed_values = state
    attended = summed_values / totals[:, :, None]
    attended = (
        jnp.transpose(attended, (1, 0, 2)).reshape(row_count, local_width).astype(jnp.bfloat16)
    )
    partial_value = jnp.dot(attended, out_weight, preferred_element_type=jnp.float32)
    return lax.psum_scatter(
        partial_value.astype(jnp.bfloat16), "head", scatter_dimension=1, tiled=True
    )


def arrange_kernel(place_ref, *refs):
    own = refs[:GROUP]
    right, left, seam, spread, sems = refs[GROUP:]
    member = place_ref[0]
    rows = right.shape[2]
    jobs = [(right.at[j], 1 + j) for j in range(3)]
    jobs += [(left.at[j], j) for j in range(3)]
    jobs += [(seam.at[j], 1 + j) for j in range(2)]
    jobs += [(spread.at[:, pl.ds(0, rows)], place_ref[1])]
    for j in range(OWNERS - 2):
        jobs += [(spread.at[:, pl.ds(rows + j * REF_DEV, REF_DEV)], place_ref[2 + j])]

    def source(m, dst):
        return own[m].at[pl.ds(0, 2), pl.ds(0, dst.shape[1])]

    for n, (dst, block) in enumerate(jobs):
        for m in range(GROUP):

            @pl.when((block ^ member) == m)
            def _():
                pltpu.make_async_copy(source(m, dst), dst, sems.at[n]).start()

    for n, (dst, _) in enumerate(jobs):
        pltpu.make_async_copy(source(0, dst), dst, sems.at[n]).wait()


def arrange(place, own, rows):
    width = own[0].shape[2]
    any_spec = pl.BlockSpec(memory_space=pl.ANY)
    spread_rows = rows + (OWNERS - 2) * REF_DEV
    shapes = [(3, 2, rows, width), (3, 2, rows, width), (2, 2, rows, width), (2, spread_rows, width)]
    return pl.pallas_call(
        arrange_kernel,
        out_shape=[jax.ShapeDtypeStruct(shape, BF16) for shape in shapes],
        in_specs=[pl.BlockSpec(memory_space=pltpu.SMEM)] + [any_spec] * GROUP,
        out_specs=[pl.BlockSpec(memory_space=pltpu.VMEM)] * len(shapes),
        scratch_shapes=[pltpu.SemaphoreType.DMA((11,))],
        compiler_params=pltpu.CompilerParams(vmem_limit_bytes=40 << 20),
        cost_estimate=pl.CostEstimate(flops=0, bytes_accessed=0, transcendentals=0),
        name="arrange_blocks",
    )(place, *own)


def attend_kernel(heads, plan, first, last, flags_ref, *refs):
    slots = sum(len(views) for views in plan)
    q_in = refs[:GROUP]
    ins = refs[GROUP : GROUP + len(plan)]
    rest = refs[GROUP + len(plan) :]
    if not first:
        state_in, rest = rest[:3], rest[3:]
    outs, rest = rest[: GROUP if last else 3], rest[GROUP if last else 3 :]
    q_buf, kv_buf, vt_buf, todo, peak, total, acc, q_sem, kv_sem, state_sem = rest
    rows = q_buf.shape[1]
    width = heads * HD
    scale = HD**-0.5 * LOG2E
    copies = [
        pltpu.make_async_copy(q_in[m].at[2, pl.ds(0, rows)], q_buf.at[m], q_sem.at[m])
        for m in range(GROUP)
    ]
    if first:
        peak[...] = jnp.full(peak.shape, NEG, F32)
        total[...] = jnp.zeros(total.shape, F32)
        acc[...] = jnp.zeros(acc.shape, F32)
    else:
        for n, buf in enumerate((peak, total, acc)):
            copies.append(pltpu.make_async_copy(state_in[n], buf, state_sem.at[n]))
    slot = 0
    for ref, views in zip(ins, plan):
        for j, first_row, held_rows in views:
            view = ref if j is None else ref.at[j]
            view = view.at[pl.ds(0, 2), pl.ds(first_row, held_rows)]
            target = kv_buf.at[slot, :, pl.ds(0, held_rows)]
            copies.append(pltpu.make_async_copy(view, target, kv_sem.at[slot]))
            if held_rows < rows:
                kv_buf[slot, :, pl.ds(held_rows, rows - held_rows)] = jnp.zeros(
                    (2, rows - held_rows, width), BF16
                )
            slot += 1
    for copy in copies:
        copy.start()

    counts = []
    for m in range(GROUP):

        def note(s, at):
            todo[m, at] = s
            return at + jnp.where(flags_ref[m, s] > 0, 1, 0)

        count = lax.fori_loop(0, slots, note, 0)
        todo[m, count] = -1
        counts.append(count)
    for copy in copies:
        copy.wait()

    def turn(s, _):
        for h in range(heads):
            vt_buf[s, h] = kv_buf[s, 1, :, pl.ds(h * HD, HD)].T
        return 0

    lax.fori_loop(0, slots, turn, 0)
    ends = (0, REF_DEV, rows)

    def one_query(m):
        def pair(p, _):
            chosen = []
            for e in range(2):
                s = todo[m, 2 * p + e]
                shut = s < 0
                s = jnp.maximum(s, 0)
                flag = jnp.where(shut, 0, flags_ref[m, s])
                some = jnp.where(flag == 3, 1.0, jnp.where(flag == 0, NEG, 0.0))
                other = jnp.where((flag & 1) == 1, 0.0, NEG)
                chosen.append((s, (some, other)))
            for h in range(heads):
                cols = pl.ds(h * HD, HD)
                q = q_buf[m, :, cols]
                new = peak[m, h]
                scores = []
                for s, bias in chosen:
                    for part in range(2):
                        k = kv_buf[s, 0, pl.ds(ends[part], ends[part + 1] - ends[part]), cols]
                        raw = (
                            lax.dot_general(
                                k, q, (((1,), (1,)), ((), ())), preferred_element_type=F32
                            )
                            * scale
                        )
                        new = jnp.maximum(new, jnp.max(raw, axis=0, keepdims=True) + bias[part])
                        scores.append((raw, bias[part]))
                keep = jnp.exp2(peak[m, h] - new)
                sums = total[m, h] * keep
                out = acc[m, h] * keep
                for e, (s, _) in enumerate(chosen):
                    weights = []
                    for raw, bias in scores[2 * e : 2 * e + 2]:
                        weight = jnp.exp2(raw - (new - bias))
                        sums = sums + jnp.sum(weight, axis=0, keepdims=True)
                        weights.append(weight.astype(BF16))
                    out = out + jnp.dot(
                        vt_buf[s, h], jnp.concatenate(weights, axis=0), preferred_element_type=F32
                    )
                peak[m, h] = new
                total[m, h] = sums
                acc[m, h] = out
            return 0

        lax.fori_loop(0, (counts[m] + 1) // 2, pair, 0)

    for m in range(GROUP):
        one_query(m)
    if last:
        for m in range(GROUP):
            for h in range(heads):
                outs[m][:, pl.ds(h * HD, HD)] = (acc[m, h] / total[m, h]).T.astype(BF16)
    else:
        for out, buf in zip(outs, (peak, total, acc)):
            out[...] = buf[...]


def attend(flags, own, rows, held, state, last):
    width = own[0].shape[2]
    heads = width // HD
    plan = tuple(tuple(views) for _, views in held)
    slots = sum(len(views) for views in plan)
    any_spec = pl.BlockSpec(memory_space=pl.ANY)
    vmem_spec = pl.BlockSpec(memory_space=pltpu.VMEM)
    state_shapes = [(GROUP, heads, 1, rows)] * 2 + [(GROUP, heads, HD, rows)]
    if last:
        out_shape = [jax.ShapeDtypeStruct((rows, width), BF16)] * GROUP
    else:
        out_shape = [jax.ShapeDtypeStruct(shape, F32) for shape in state_shapes]
    state = state or []
    return pl.pallas_call(
        functools.partial(attend_kernel, heads, plan, not state, last),
        out_shape=out_shape,
        in_specs=[pl.BlockSpec(memory_space=pltpu.SMEM)]
        + [any_spec] * (GROUP + len(held) + len(state)),
        out_specs=[vmem_spec] * len(out_shape),
        scratch_shapes=[
            pltpu.VMEM((GROUP, rows, width), BF16),
            pltpu.VMEM((slots, 2, rows, width), BF16),
            pltpu.VMEM((slots, heads, HD, rows), BF16),
            pltpu.SMEM((GROUP, slots + 2), jnp.int32),
        ]
        + [pltpu.VMEM(shape, F32) for shape in state_shapes]
        + [
            pltpu.SemaphoreType.DMA((GROUP,)),
            pltpu.SemaphoreType.DMA((slots,)),
            pltpu.SemaphoreType.DMA((3,)),
        ],
        compiler_params=pltpu.CompilerParams(vmem_limit_bytes=48 << 20),
        cost_estimate=pl.CostEstimate(flops=0, bytes_accessed=0, transcendentals=0),
        name="attend_slots",
    )(flags, *own, *[array for array, _ in held], *state)


def grouped_body(query_rows, key_rows, value_rows, pattern, owners, out_weight):
    rows, width = query_rows.shape
    local_heads = width // HD
    out_cols = out_weight.shape[1] // 2
    blocks = GROUP * PLANES
    top = PLANES - 1
    index = lax.axis_index("seq")
    side = lax.axis_index("head")
    plane, member = index // GROUP, index % GROUP
    per_member = local_heads // GROUP
    chunks = CHUNKS if sum(CHUNKS) == per_member else (per_member,)
    starts = [sum(chunks[:c]) for c in range(len(chunks))]

    def swap(value, m):
        return lax.ppermute(value, "seq", [(i, i ^ m) for i in range(blocks)])

    def hop(value, pairs):
        moves = [(a * GROUP + g, b * GROUP + g) for a, b in pairs for g in range(GROUP)]
        return lax.ppermute(value, "seq", moves)

    def across(value):
        return lax.ppermute(value, "head", [(0, 1), (1, 0)])

    def split_heads(start, heads):
        pieces = []
        note = jnp.pad(
            (pattern != 0).astype(BF16)[None],
            ((0, 2), (rows, PAT_ROWS - 1), (0, heads * HD - 2 * REACH)),
        )
        for m in range(GROUP):
            first = (GROUP * start + (member ^ m) * heads) * HD
            piece = jnp.stack(
                [
                    lax.dynamic_slice_in_dim(array, first, heads * HD, 1)
                    for array in (key_rows, value_rows, query_rows)
                ]
            )
            piece = jnp.pad(piece, ((0, 0), (0, PAT_ROWS), (0, 0))) + note
            pieces.append(piece if m == 0 else swap(piece, m))
        return pieces

    inner = (owners != 0) & (owners != blocks - 1)
    owner_a = jnp.min(jnp.where(inner, owners, blocks))
    owner_b = jnp.max(jnp.where(inner, owners, -1))
    place = jnp.stack(
        [
            member,
            jnp.where(plane == 0, 0, GROUP - 1),
            owner_a % GROUP,
            owner_b % GROUP,
        ]
    ).astype(jnp.int32)
    homes = (owner_a // GROUP, owner_b // GROUP)

    ups = [(p, p + 1) for p in range(top)]
    downs = [(p + 1, p) for p in range(top)]
    row = jnp.arange(rows + (OWNERS - 2) * REF_DEV, dtype=jnp.int32)
    keep_own = (row >= rows) & (row < rows + REF_DEV) & (plane == homes[0])
    keep_own = keep_own | ((row >= rows + REF_DEV) & (plane == homes[1]))
    keep_own = keep_own[None, :, None]
    own_all, near_all, seams, spreads = [], [], [], []
    for c, heads in enumerate(chunks):
        own = split_heads(starts[c], heads)
        right, left, seam, sent = arrange(place, own, rows)
        if c == 0:
            right, out_weight = lax.optimization_barrier((right, out_weight))
        arrived = []
        value = sent
        for n in range(top):
            value = hop(value, [(n, n + 1), (top - n, top - n - 1)])
            arrived.append(value)
            value = jnp.where(keep_own, sent, value)
        near_all.append((hop(right, ups), hop(left, downs)))
        seams.append(hop(seam, [(0, top), (top, 0)]))
        own_all.append(own)
        spreads.append(arrived)

    my_blocks = plane * GROUP + (jnp.arange(GROUP, dtype=jnp.int32) ^ member)
    base = plane * GROUP
    three = jnp.arange(3, dtype=jnp.int32)
    is_end = (plane == 0) | (plane == top)
    low_end, high_end = jnp.int32(0), jnp.int32(blocks - 1)
    held = jnp.concatenate(
        [
            my_blocks,
            jnp.where(plane > 0, base - 3 + three, -1),
            jnp.where(plane < top, base + GROUP + three, -1),
            jnp.where(is_end, jnp.where(plane == 0, blocks - 3, 1) + three[:2], -1),
            jnp.stack(
                [
                    jnp.where(is_end, -1, jnp.where(plane == 1, low_end, high_end)),
                    jnp.where(is_end, -1, jnp.where(plane == 1, high_end, low_end)),
                    jnp.where(is_end, jnp.where(plane == 0, high_end, low_end), -1),
                ]
            ),
        ]
    )
    my_pattern = jnp.stack([own[0, rows, : 2 * REACH] for own in own_all[0]])
    away = (held[None, :] - my_blocks[:, None]) % blocks
    full = (away == 0).astype(jnp.int32)
    for offset in list(range(-REACH, 0)) + list(range(1, REACH + 1)):
        chosen = (my_pattern[:, column_of(offset)] != 0)[:, None]
        full = full + (chosen & (away == offset % blocks)).astype(jnp.int32)
    is_ref = (held == 0) | (held == blocks - 1)
    is_own = jnp.arange(held.shape[0]) < GROUP
    is_ref = is_ref | (is_own & ((held == owner_a) | (held == owner_b)))
    flags = jnp.where(held >= 0, full + 2 * is_ref.astype(jnp.int32), 0)
    far_flags = [flags[:, -5:-3]]
    for n in range(top):
        comes = [flags[:, n - 3][:, None]]
        for home in homes:
            if n == 0:
                here = ((plane == 1) & (home == 0)) | ((plane == 2) & (home == 3))
            elif n == 1:
                here = ((plane == 1) & (home >= 2)) | ((plane == 2) & (home <= 1))
            else:
                here = ((plane == 0) & (home > 0)) | ((plane == 3) & (home < 3))
            comes.append(jnp.broadcast_to(jnp.where(here, 2, 0), (GROUP, 1)))
        far_flags += comes
    far_flags = jnp.concatenate(far_flags, axis=1).astype(jnp.int32)
    near_flags = flags[:, : GROUP + 6]

    half = width // 2
    core = index % 2
    theirs = lax.dynamic_slice(out_weight, (core * half, (1 - side) * out_cols), (half, out_cols))
    part = across(theirs)
    rest = swap(part, 1)
    weight_far = jnp.where(core == 0, jnp.concatenate([part, rest]), jnp.concatenate([rest, part]))
    weight_near = lax.dynamic_slice_in_dim(out_weight, side * out_cols, out_cols, 1)

    mixed = jnp.zeros((rows, out_cols), F32)
    for c, heads in enumerate(chunks):
        own = own_all[c]
        several = [(j, 0, rows) for j in range(3)]
        state = attend(
            near_flags,
            own,
            rows,
            [(array, [(None, 0, rows)]) for array in own]
            + [(array, several) for array in near_all[c]],
            None,
            False,
        )
        parts = [(None, 0, rows)]
        parts += [(None, rows + j * REF_DEV, REF_DEV) for j in range(OWNERS - 2)]
        outs = attend(
            far_flags,
            own,
            rows,
            [(seams[c], several[:2])] + [(array, parts) for array in spreads[c]],
            list(state),
            True,
        )
        near = jnp.concatenate([outs[0]] + [swap(outs[m], m) for m in range(1, GROUP)], axis=1)
        far = across(near)

        def weight_rows(weight):
            return jnp.concatenate(
                [
                    lax.dynamic_slice_in_dim(
                        weight, (GROUP * starts[c] + (member ^ m) * heads) * HD, heads * HD, 0
                    )
                    for m in range(GROUP)
                ]
            )

        mixed = mixed + jnp.dot(near, weight_rows(weight_near), preferred_element_type=F32)
        mixed = mixed + jnp.dot(far, weight_rows(weight_far), preferred_element_type=F32)
    return mixed.astype(BF16)


def body(query_rows, key_rows, value_rows, pattern, owners, out_weight):
    fits = (
        lax.axis_size("seq") == GROUP * PLANES
        and lax.axis_size("head") == 2
        and (query_rows.shape[1] // HD) % GROUP == 0
    )
    plan = grouped_body if fits else plain_body
    return plan(query_rows, key_rows, value_rows, pattern, owners, out_weight)


def solution(mesh):
    return jax.shard_map(
        body,
        mesh=mesh,
        in_specs=(
            P("seq", "head"),
            P("seq", "head"),
            P("seq", "head"),
            P("seq", None),
            P(),
            P("head", None),
        ),
        out_specs=P("seq", "head"),
        check_vma=False,
    )
```

```python
import functools

import jax
import jax.numpy as jnp
from jax import lax
from jax.experimental import pallas as pl
from jax.experimental.pallas import tpu as pltpu
from jax.sharding import PartitionSpec as P

HD = 128
REACH = 3
OWNERS = 4
REF_DEV = 256
GROUP = 4
PLANES = 4
CHUNKS = (2, 1)
PAT_ROWS = 16
NEG = -1e30
LOG2E = 1.4426950408889634
F32 = jnp.float32
BF16 = jnp.bfloat16


def broadcast(block, axis, owner):
    block = jnp.where(lax.axis_index(axis) == owner, block, jnp.zeros_like(block))
    return lax.psum(block, axis)


def from_behind(value, axis, steps):
    count = lax.axis_size(axis)
    pairs = [(source, (source + steps) % count) for source in range(count)]
    return lax.ppermute(value, axis, pairs)


def column_of(offset):
    return offset + REACH if offset < 0 else offset + REACH - 1


def merge_block(state, query_three, block_keys, block_values):
    peaks, totals, summed_values = state
    local_heads = query_three.shape[1]
    keys_three = block_keys.reshape(-1, local_heads, HD)
    values_three = block_values.reshape(-1, local_heads, HD)
    scores = jnp.einsum(
        "qhd,khd->hqk", query_three, keys_three, preferred_element_type=jnp.float32
    ) * HD ** (-0.5)
    new_peaks = jnp.maximum(peaks, jnp.max(scores, axis=-1))
    rescale = jnp.exp(peaks - new_peaks)
    weights = jnp.exp(scores - new_peaks[:, :, None])
    totals = totals * rescale + jnp.sum(weights, axis=-1)
    contrib = jnp.einsum(
        "hqk,khd->hqd",
        weights.astype(jnp.bfloat16),
        values_three,
        preferred_element_type=jnp.float32,
    )
    summed_values = summed_values * rescale[:, :, None] + contrib
    return (new_peaks, totals, summed_values)


def absorb(state, query_three, stacked, active):
    return lax.cond(
        active,
        lambda inner: merge_block(inner, query_three, stacked[0], stacked[1]),
        lambda inner: inner,
        state,
    )


def plain_body(query_rows, key_rows, value_rows, pattern, owners, out_weight):
    row_count = query_rows.shape[0]
    local_width = query_rows.shape[1]
    local_heads = local_width // HD
    query_three = query_rows.reshape(row_count, local_heads, HD)
    start_state = (
        jnp.full((local_heads, row_count), -jnp.inf, jnp.float32),
        jnp.zeros((local_heads, row_count), jnp.float32),
        jnp.zeros((local_heads, row_count, HD), jnp.float32),
    )
    state = merge_block(start_state, query_three, key_rows, value_rows)
    own_stack = jnp.stack([key_rows, value_rows])
    ref_stack = jnp.stack([key_rows[:REF_DEV], value_rows[:REF_DEV]])
    for member in range(OWNERS):
        arrived = broadcast(ref_stack, "seq", owners[member])
        state = merge_block(state, query_three, arrived[0], arrived[1])
    for distance in range(1, REACH + 1):
        for offset in (-distance, distance):
            arrived = from_behind(own_stack, "seq", -offset)
            state = absorb(state, query_three, arrived, pattern[0, column_of(offset)] != 0)
    peaks, totals, summed_values = state
    attended = summed_values / totals[:, :, None]
    attended = (
        jnp.transpose(attended, (1, 0, 2)).reshape(row_count, local_width).astype(jnp.bfloat16)
    )
    partial_value = jnp.dot(attended, out_weight, preferred_element_type=jnp.float32)
    return lax.psum_scatter(
        partial_value.astype(jnp.bfloat16), "head", scatter_dimension=1, tiled=True
    )


def attend_kernel(heads, plan, first, last, flags_ref, *refs):
    slots = sum(plan)
    q_in = refs[:GROUP]
    ins = refs[GROUP : GROUP + len(plan)]
    rest = refs[GROUP + len(plan) :]
    if not first:
        state_in, rest = rest[:3], rest[3:]
    outs, rest = rest[: GROUP if last else 3], rest[GROUP if last else 3 :]
    q_buf, kv_buf, vt_buf, todo, peak, total, acc, q_sem, kv_sem, state_sem = rest
    rows = q_buf.shape[1]
    width = heads * HD
    scale = HD**-0.5 * LOG2E
    copies = [
        pltpu.make_async_copy(q_in[m].at[2, pl.ds(0, rows)], q_buf.at[m], q_sem.at[m])
        for m in range(GROUP)
    ]
    if first:
        peak[...] = jnp.full(peak.shape, NEG, F32)
        total[...] = jnp.zeros(total.shape, F32)
        acc[...] = jnp.zeros(acc.shape, F32)
    else:
        for n, buf in enumerate((peak, total, acc)):
            copies.append(pltpu.make_async_copy(state_in[n], buf, state_sem.at[n]))
    slot = 0
    for ref, count in zip(ins, plan):
        for j in range(count):
            copies.append(pltpu.make_async_copy(ref.at[j], kv_buf.at[slot], kv_sem.at[slot]))
            slot += 1
    for copy in copies:
        copy.start()

    counts = []
    for m in range(GROUP):

        def note(s, at):
            todo[m, at] = s
            return at + jnp.where(flags_ref[m, s] > 0, 1, 0)

        count = lax.fori_loop(0, slots, note, 0)
        todo[m, count] = -1
        counts.append(count)
    for copy in copies:
        copy.wait()

    def turn(s, _):
        for h in range(heads):
            vt_buf[s, h] = kv_buf[s, 1, :, pl.ds(h * HD, HD)].T
        return 0

    lax.fori_loop(0, slots, turn, 0)
    ends = (0, REF_DEV, rows)

    def one_query(m):
        def pair(p, _):
            chosen = []
            for e in range(2):
                s = todo[m, 2 * p + e]
                shut = s < 0
                s = jnp.maximum(s, 0)
                flag = jnp.where(shut, 0, flags_ref[m, s])
                some = jnp.where(flag == 3, 1.0, jnp.where(flag == 0, NEG, 0.0))
                other = jnp.where((flag & 1) == 1, 0.0, NEG)
                chosen.append((s, (some, other)))
            for h in range(heads):
                cols = pl.ds(h * HD, HD)
                q = q_buf[m, :, cols]
                new = peak[m, h]
                scores = []
                for s, bias in chosen:
                    for part in range(2):
                        k = kv_buf[s, 0, pl.ds(ends[part], ends[part + 1] - ends[part]), cols]
                        raw = (
                            lax.dot_general(
                                k, q, (((1,), (1,)), ((), ())), preferred_element_type=F32
                            )
                            * scale
                        )
                        new = jnp.maximum(new, jnp.max(raw, axis=0, keepdims=True) + bias[part])
                        scores.append((raw, bias[part]))
                keep = jnp.exp2(peak[m, h] - new)
                sums = total[m, h] * keep
                out = acc[m, h] * keep
                for e, (s, _) in enumerate(chosen):
                    weights = []
                    for raw, bias in scores[2 * e : 2 * e + 2]:
                        weight = jnp.exp2(raw - (new - bias))
                        sums = sums + jnp.sum(weight, axis=0, keepdims=True)
                        weights.append(weight.astype(BF16))
                    out = out + jnp.dot(
                        vt_buf[s, h], jnp.concatenate(weights, axis=0), preferred_element_type=F32
                    )
                peak[m, h] = new
                total[m, h] = sums
                acc[m, h] = out
            return 0

        lax.fori_loop(0, (counts[m] + 1) // 2, pair, 0)

    for m in range(GROUP):
        one_query(m)
    if last:
        for m in range(GROUP):
            for h in range(heads):
                outs[m][:, pl.ds(h * HD, HD)] = (acc[m, h] / total[m, h]).T.astype(BF16)
    else:
        for out, buf in zip(outs, (peak, total, acc)):
            out[...] = buf[...]


def attend(flags, own, held, state, last):
    rows, width = held[0].shape[2:]
    heads = width // HD
    plan = tuple(array.shape[0] for array in held)
    slots = sum(plan)
    any_spec = pl.BlockSpec(memory_space=pl.ANY)
    vmem_spec = pl.BlockSpec(memory_space=pltpu.VMEM)
    state_shapes = [(GROUP, heads, 1, rows)] * 2 + [(GROUP, heads, HD, rows)]
    if last:
        out_shape = [jax.ShapeDtypeStruct((rows, width), BF16)] * GROUP
    else:
        out_shape = [jax.ShapeDtypeStruct(shape, F32) for shape in state_shapes]
    state = state or []
    return pl.pallas_call(
        functools.partial(attend_kernel, heads, plan, not state, last),
        out_shape=out_shape,
        in_specs=[pl.BlockSpec(memory_space=pltpu.SMEM)]
        + [any_spec] * (GROUP + len(held) + len(state)),
        out_specs=[vmem_spec] * len(out_shape),
        scratch_shapes=[
            pltpu.VMEM((GROUP, rows, width), BF16),
            pltpu.VMEM((slots, 2, rows, width), BF16),
            pltpu.VMEM((slots, heads, HD, rows), BF16),
            pltpu.SMEM((GROUP, slots + 2), jnp.int32),
        ]
        + [pltpu.VMEM(shape, F32) for shape in state_shapes]
        + [
            pltpu.SemaphoreType.DMA((GROUP,)),
            pltpu.SemaphoreType.DMA((slots,)),
            pltpu.SemaphoreType.DMA((3,)),
        ],
        compiler_params=pltpu.CompilerParams(vmem_limit_bytes=48 << 20),
        cost_estimate=pl.CostEstimate(flops=0, bytes_accessed=0, transcendentals=0),
        name="attend_slots",
    )(flags, *own, *held, *state)


def grouped_body(query_rows, key_rows, value_rows, pattern, owners, out_weight):
    rows, width = query_rows.shape
    out_cols = out_weight.shape[1] // 2
    blocks = GROUP * PLANES
    index = lax.axis_index("seq")
    side = lax.axis_index("head")
    plane, member = index // GROUP, index % GROUP
    per_plane = width // HD // PLANES
    chunks = CHUNKS if sum(CHUNKS) == per_plane else (per_plane,)
    starts = [sum(chunks[:c]) for c in range(len(chunks))]

    def swap(value, bits):
        return lax.ppermute(value, "seq", [(i, i ^ bits) for i in range(blocks)])

    def swap_planes(value, k):
        return swap(value, GROUP * k)

    def across(value):
        return lax.ppermute(value, "head", [(0, 1), (1, 0)])

    def after(value, *others):
        return lax.optimization_barrier((value, others))[0]

    def pack_heads(arrays, start, heads):
        note = jnp.pad(
            (pattern != 0).astype(BF16)[None],
            ((0, 2), (rows, PAT_ROWS - 1), (0, heads * HD - 2 * REACH)),
        )
        pieces = []
        for k in range(PLANES):
            first = ((plane ^ k) * per_plane + start) * HD
            piece = jnp.stack(
                [lax.dynamic_slice_in_dim(array, first, heads * HD, 1) for array in arrays]
            )
            pieces.append(jnp.pad(piece, ((0, 0), (0, PAT_ROWS), (0, 0))) + note)
        return pieces

    arrays = (key_rows, value_rows, query_rows)
    half = width // 2
    core = index % 2
    packed = [pack_heads(arrays, starts[0], chunks[0])]
    weight = after(out_weight, packed[0])
    theirs = lax.dynamic_slice(weight, (core * half, (1 - side) * out_cols), (half, out_cols))
    part = across(theirs)
    for c in range(1, len(chunks)):
        arrays = after(arrays, packed[-1], theirs)
        packed.append(pack_heads(arrays, starts[c], chunks[c]))

    pieces_all, shared = [], []
    for c in range(len(chunks)):
        pieces = packed[c]
        if c > 0:
            before = pieces_all[-1]
            pieces = [
                pieces[0],
                after(pieces[1], before[3]),
                after(pieces[2], before[2]),
                after(pieces[3], before[1]),
            ]
        pieces = [pieces[0]] + [swap_planes(pieces[k], k) for k in range(1, PLANES)]
        mine = jnp.stack([piece[:2, :rows] for piece in pieces])
        beside = swap(mine, 1)
        chip = swap(mine, 2)
        chip_beside = swap(chip, 1)
        pieces_all.append(pieces)
        shared.append((mine, beside, chip, chip_beside))

    planes_at = (plane ^ jnp.arange(PLANES, dtype=jnp.int32)) * GROUP
    my_blocks = planes_at + member
    held = jnp.concatenate([planes_at + (member ^ m) for m in range(GROUP)])
    my_pattern = jnp.stack([piece[0, rows, : 2 * REACH] for piece in pieces_all[0]])
    away = (held[None, :] - my_blocks[:, None]) % blocks
    full = (away == 0).astype(jnp.int32)
    for offset in list(range(-REACH, 0)) + list(range(1, REACH + 1)):
        chosen = (my_pattern[:, column_of(offset)] != 0)[:, None]
        full = full + (chosen & (away == offset % blocks)).astype(jnp.int32)
    is_ref = jnp.any(held[:, None] == owners[None, :], axis=1).astype(jnp.int32)
    flags = full + 2 * is_ref[None, :]
    near_flags, far_flags = flags[:, : 2 * PLANES], flags[:, 2 * PLANES :]

    def weight_rows(weight, start, heads):
        return jnp.concatenate(
            [
                lax.dynamic_slice_in_dim(
                    weight, ((plane ^ k) * per_plane + start) * HD, heads * HD, 0
                )
                for k in range(PLANES)
            ]
        )

    mixed = jnp.zeros((rows, out_cols), F32)
    weights = []
    done = []
    for c in range(len(chunks)):
        own = pieces_all[c]
        mine, beside, chip, chip_beside = shared[c]
        if c > 0:
            own = after(own, done[-1])
        state = attend(near_flags, own, [mine, beside], None, False)
        if c == 0:
            part = after(part, state)
            rest = swap(part, 1)
            weight_far = jnp.where(
                core == 0, jnp.concatenate([part, rest]), jnp.concatenate([rest, part])
            )
            weight_near = lax.dynamic_slice_in_dim(out_weight, side * out_cols, out_cols, 1)
            weights = [
                [weight_rows(weight, starts[n], chunks[n]) for weight in (weight_near, weight_far)]
                for n in range(len(chunks))
            ]
        else:
            state = after(state, weights)
        outs = attend(far_flags, own, [chip, chip_beside], list(state), True)
        done.append(outs)
        near = jnp.concatenate(
            [outs[0]] + [swap_planes(outs[k], k) for k in range(1, PLANES)], axis=1
        )
        far = across(near)
        weight_n, weight_f = weights[c]
        mixed = mixed + jnp.dot(near, weight_n, preferred_element_type=F32)
        mixed = mixed + jnp.dot(far, weight_f, preferred_element_type=F32)
    return mixed.astype(BF16)


def body(query_rows, key_rows, value_rows, pattern, owners, out_weight):
    fits = (
        lax.axis_size("seq") == GROUP * PLANES
        and lax.axis_size("head") == 2
        and (query_rows.shape[1] // HD) % PLANES == 0
    )
    plan = grouped_body if fits else plain_body
    return plan(query_rows, key_rows, value_rows, pattern, owners, out_weight)


def solution(mesh):
    return jax.shard_map(
        body,
        mesh=mesh,
        in_specs=(
            P("seq", "head"),
            P("seq", "head"),
            P("seq", "head"),
            P("seq", None),
            P(),
            P("head", None),
        ),
        out_specs=P("seq", "head"),
        check_vma=False,
    )
```

```python
import functools

import jax
import jax.numpy as jnp
from jax import lax
from jax.experimental import pallas as pl
from jax.experimental.pallas import tpu as pltpu
from jax.sharding import PartitionSpec as P

HD = 128
REACH = 3
OWNERS = 4
REF_DEV = 256
GROUP = 4
PLANES = 4
CHUNKS = (2, 1)
PAT_ROWS = 16
NEG = -1e30
LOG2E = 1.4426950408889634
F32 = jnp.float32
BF16 = jnp.bfloat16


def broadcast(block, axis, owner):
    block = jnp.where(lax.axis_index(axis) == owner, block, jnp.zeros_like(block))
    return lax.psum(block, axis)


def from_behind(value, axis, steps):
    count = lax.axis_size(axis)
    pairs = [(source, (source + steps) % count) for source in range(count)]
    return lax.ppermute(value, axis, pairs)


def column_of(offset):
    return offset + REACH if offset < 0 else offset + REACH - 1


def merge_block(state, query_three, block_keys, block_values):
    peaks, totals, summed_values = state
    local_heads = query_three.shape[1]
    keys_three = block_keys.reshape(-1, local_heads, HD)
    values_three = block_values.reshape(-1, local_heads, HD)
    scores = jnp.einsum(
        "qhd,khd->hqk", query_three, keys_three, preferred_element_type=jnp.float32
    ) * HD ** (-0.5)
    new_peaks = jnp.maximum(peaks, jnp.max(scores, axis=-1))
    rescale = jnp.exp(peaks - new_peaks)
    weights = jnp.exp(scores - new_peaks[:, :, None])
    totals = totals * rescale + jnp.sum(weights, axis=-1)
    contrib = jnp.einsum(
        "hqk,khd->hqd",
        weights.astype(jnp.bfloat16),
        values_three,
        preferred_element_type=jnp.float32,
    )
    summed_values = summed_values * rescale[:, :, None] + contrib
    return (new_peaks, totals, summed_values)


def absorb(state, query_three, stacked, active):
    return lax.cond(
        active,
        lambda inner: merge_block(inner, query_three, stacked[0], stacked[1]),
        lambda inner: inner,
        state,
    )


def plain_body(query_rows, key_rows, value_rows, pattern, owners, out_weight):
    row_count = query_rows.shape[0]
    local_width = query_rows.shape[1]
    local_heads = local_width // HD
    query_three = query_rows.reshape(row_count, local_heads, HD)
    start_state = (
        jnp.full((local_heads, row_count), -jnp.inf, jnp.float32),
        jnp.zeros((local_heads, row_count), jnp.float32),
        jnp.zeros((local_heads, row_count, HD), jnp.float32),
    )
    state = merge_block(start_state, query_three, key_rows, value_rows)
    own_stack = jnp.stack([key_rows, value_rows])
    ref_stack = jnp.stack([key_rows[:REF_DEV], value_rows[:REF_DEV]])
    for member in range(OWNERS):
        arrived = broadcast(ref_stack, "seq", owners[member])
        state = merge_block(state, query_three, arrived[0], arrived[1])
    for distance in range(1, REACH + 1):
        for offset in (-distance, distance):
            arrived = from_behind(own_stack, "seq", -offset)
            state = absorb(state, query_three, arrived, pattern[0, column_of(offset)] != 0)
    peaks, totals, summed_values = state
    attended = summed_values / totals[:, :, None]
    attended = (
        jnp.transpose(attended, (1, 0, 2)).reshape(row_count, local_width).astype(jnp.bfloat16)
    )
    partial_value = jnp.dot(attended, out_weight, preferred_element_type=jnp.float32)
    return lax.psum_scatter(
        partial_value.astype(jnp.bfloat16), "head", scatter_dimension=1, tiled=True
    )


def attend_kernel(heads, plan, first, last, flags_ref, *refs):
    slots = sum(plan)
    q_in = refs[:GROUP]
    ins = refs[GROUP : GROUP + len(plan)]
    rest = refs[GROUP + len(plan) :]
    if not first:
        state_in, rest = rest[:3], rest[3:]
    outs, rest = rest[: GROUP if last else 3], rest[GROUP if last else 3 :]
    q_buf, kv_buf, vt_buf, todo, peak, total, acc, q_sem, kv_sem, state_sem = rest
    rows = q_buf.shape[1]
    width = heads * HD
    scale = HD**-0.5 * LOG2E
    copies = [
        pltpu.make_async_copy(q_in[m].at[2, pl.ds(0, rows)], q_buf.at[m], q_sem.at[m])
        for m in range(GROUP)
    ]
    if first:
        peak[...] = jnp.full(peak.shape, NEG, F32)
        total[...] = jnp.zeros(total.shape, F32)
        acc[...] = jnp.zeros(acc.shape, F32)
    else:
        for n, buf in enumerate((peak, total, acc)):
            copies.append(pltpu.make_async_copy(state_in[n], buf, state_sem.at[n]))
    slot = 0
    for ref, count in zip(ins, plan):
        for j in range(count):
            copies.append(pltpu.make_async_copy(ref.at[j], kv_buf.at[slot], kv_sem.at[slot]))
            slot += 1
    for copy in copies:
        copy.start()

    counts = []
    for m in range(GROUP):

        def note(s, at):
            todo[m, at] = s
            return at + jnp.where(flags_ref[m, s] > 0, 1, 0)

        count = lax.fori_loop(0, slots, note, 0)
        todo[m, count] = -1
        counts.append(count)
    for copy in copies:
        copy.wait()

    def turn(s, _):
        for h in range(heads):
            vt_buf[s, h] = kv_buf[s, 1, :, pl.ds(h * HD, HD)].T
        return 0

    lax.fori_loop(0, slots, turn, 0)
    ends = (0, REF_DEV, rows)

    def one_query(m):
        def pair(p, _):
            chosen = []
            for e in range(2):
                s = todo[m, 2 * p + e]
                shut = s < 0
                s = jnp.maximum(s, 0)
                flag = jnp.where(shut, 0, flags_ref[m, s])
                some = jnp.where(flag == 3, 1.0, jnp.where(flag == 0, NEG, 0.0))
                other = jnp.where((flag & 1) == 1, 0.0, NEG)
                chosen.append((s, (some, other)))
            for h in range(heads):
                cols = pl.ds(h * HD, HD)
                q = q_buf[m, :, cols]
                new = peak[m, h]
                scores = []
                for s, bias in chosen:
                    for part in range(2):
                        k = kv_buf[s, 0, pl.ds(ends[part], ends[part + 1] - ends[part]), cols]
                        raw = (
                            lax.dot_general(
                                k, q, (((1,), (1,)), ((), ())), preferred_element_type=F32
                            )
                            * scale
                        )
                        new = jnp.maximum(new, jnp.max(raw, axis=0, keepdims=True) + bias[part])
                        scores.append((raw, bias[part]))
                keep = jnp.exp2(peak[m, h] - new)
                sums = total[m, h] * keep
                out = acc[m, h] * keep
                for e, (s, _) in enumerate(chosen):
                    weights = []
                    for raw, bias in scores[2 * e : 2 * e + 2]:
                        weight = jnp.exp2(raw - (new - bias))
                        sums = sums + jnp.sum(weight, axis=0, keepdims=True)
                        weights.append(weight.astype(BF16))
                    out = out + jnp.dot(
                        vt_buf[s, h], jnp.concatenate(weights, axis=0), preferred_element_type=F32
                    )
                peak[m, h] = new
                total[m, h] = sums
                acc[m, h] = out
            return 0

        lax.fori_loop(0, (counts[m] + 1) // 2, pair, 0)

    for m in range(GROUP):
        one_query(m)
    if last:
        for m in range(GROUP):
            for h in range(heads):
                outs[m][:, pl.ds(h * HD, HD)] = (acc[m, h] / total[m, h]).T.astype(BF16)
    else:
        for out, buf in zip(outs, (peak, total, acc)):
            out[...] = buf[...]


def attend(flags, own, held, state, last):
    rows, width = held[0].shape[2:]
    heads = width // HD
    plan = tuple(array.shape[0] for array in held)
    slots = sum(plan)
    any_spec = pl.BlockSpec(memory_space=pl.ANY)
    vmem_spec = pl.BlockSpec(memory_space=pltpu.VMEM)
    state_shapes = [(GROUP, heads, 1, rows)] * 2 + [(GROUP, heads, HD, rows)]
    if last:
        out_shape = [jax.ShapeDtypeStruct((rows, width), BF16)] * GROUP
    else:
        out_shape = [jax.ShapeDtypeStruct(shape, F32) for shape in state_shapes]
    state = state or []
    return pl.pallas_call(
        functools.partial(attend_kernel, heads, plan, not state, last),
        out_shape=out_shape,
        in_specs=[pl.BlockSpec(memory_space=pltpu.SMEM)]
        + [any_spec] * (GROUP + len(held) + len(state)),
        out_specs=[vmem_spec] * len(out_shape),
        scratch_shapes=[
            pltpu.VMEM((GROUP, rows, width), BF16),
            pltpu.VMEM((slots, 2, rows, width), BF16),
            pltpu.VMEM((slots, heads, HD, rows), BF16),
            pltpu.SMEM((GROUP, slots + 2), jnp.int32),
        ]
        + [pltpu.VMEM(shape, F32) for shape in state_shapes]
        + [
            pltpu.SemaphoreType.DMA((GROUP,)),
            pltpu.SemaphoreType.DMA((slots,)),
            pltpu.SemaphoreType.DMA((3,)),
        ],
        compiler_params=pltpu.CompilerParams(vmem_limit_bytes=20 << 20),
        cost_estimate=pl.CostEstimate(flops=0, bytes_accessed=0, transcendentals=0),
        name="attend_slots",
    )(flags, *own, *held, *state)


def grouped_body(query_rows, key_rows, value_rows, pattern, owners, out_weight):
    rows, width = query_rows.shape
    out_cols = out_weight.shape[1] // 2
    blocks = GROUP * PLANES
    index = lax.axis_index("seq")
    side = lax.axis_index("head")
    plane, member = index // GROUP, index % GROUP
    per_plane = width // HD // PLANES
    chunks = CHUNKS if sum(CHUNKS) == per_plane else (per_plane,)
    starts = [sum(chunks[:c]) for c in range(len(chunks))]

    def swap(value, bits):
        return lax.ppermute(value, "seq", [(i, i ^ bits) for i in range(blocks)])

    def swap_planes(value, k):
        return swap(value, GROUP * k)

    def across(value):
        return lax.ppermute(value, "head", [(0, 1), (1, 0)])

    def after(value, *others):
        return lax.optimization_barrier((value, others))[0]

    def stack(pieces):
        return jnp.stack([piece[:2, :rows] for piece in pieces])

    def pack_heads(arrays, start, heads):
        note = jnp.pad(
            (pattern != 0).astype(BF16)[None],
            ((0, 2), (rows, PAT_ROWS - 1), (0, heads * HD - 2 * REACH)),
        )
        pieces = []
        for k in range(PLANES):
            first = ((plane ^ k) * per_plane + start) * HD
            piece = jnp.stack(
                [lax.dynamic_slice_in_dim(array, first, heads * HD, 1) for array in arrays]
            )
            pieces.append(jnp.pad(piece, ((0, 0), (0, PAT_ROWS), (0, 0))) + note)
        return pieces

    arrays = (key_rows, value_rows, query_rows)
    half = width // 2
    core = index % 2
    packed = [pack_heads(arrays, starts[0], chunks[0])]

    def weight_rows(weight, side_at, away, c):
        return [
            lax.dynamic_slice(
                weight,
                (((plane ^ k) * per_plane + starts[c]) * HD, side_at * out_cols),
                (chunks[c] * HD, out_cols),
            )
            for k in away
        ]

    weight = after(out_weight, packed[0])
    theirs = jnp.concatenate(
        sum([weight_rows(weight, 1 - side, (2 * core, 2 * core + 1), c) for c in range(len(chunks))], [])
    )
    part = across(theirs)
    weight_near = [
        jnp.concatenate(weight_rows(after(weight, theirs), side, range(PLANES), c))
        for c in range(len(chunks))
    ]
    for c in range(1, len(chunks)):
        arrays = after(arrays, packed[-1], theirs)
        packed.append(pack_heads(arrays, starts[c], chunks[c]))

    def receive(pieces, *gate):
        pieces = [pieces[0]] + [swap_planes(pieces[k], k) for k in range(1, PLANES)]
        low = stack(pieces[:2])
        chip_low = swap(low, 2)
        pieces[2:] = after(pieces[2:], *gate) if gate else after(pieces[2:], chip_low, weight_near)
        high = stack(pieces[2:])
        chip_high = swap(high, 2)
        mine = [low, high, swap(low, 1), swap(high, 1)]
        return pieces, mine, [chip_low, chip_high, swap(chip_low, 1), swap(chip_high, 1)]

    received = [receive(packed[0])]

    planes_at = (plane ^ jnp.arange(PLANES, dtype=jnp.int32)) * GROUP
    my_blocks = planes_at + member
    held = jnp.concatenate([planes_at + (member ^ m) for m in range(GROUP)])
    my_pattern = jnp.stack([piece[0, rows, : 2 * REACH] for piece in received[0][0]])
    away = (held[None, :] - my_blocks[:, None]) % blocks
    full = (away == 0).astype(jnp.int32)
    for offset in list(range(-REACH, 0)) + list(range(1, REACH + 1)):
        chosen = (my_pattern[:, column_of(offset)] != 0)[:, None]
        full = full + (chosen & (away == offset % blocks)).astype(jnp.int32)
    is_ref = jnp.any(held[:, None] == owners[None, :], axis=1).astype(jnp.int32)
    flags = full + 2 * is_ref[None, :]
    near_flags, far_flags = flags[:, : 2 * PLANES], flags[:, 2 * PLANES :]

    def project(mixed, near, far, c, part, rest):
        mixed = mixed + jnp.dot(near, weight_near[c], preferred_element_type=F32)
        pair_width = 2 * chunks[c] * HD
        row = 2 * starts[c] * HD
        for at, held in ((core, part), (1 - core, rest)):
            columns = lax.dynamic_slice_in_dim(far, at * pair_width, pair_width, 1)
            mixed = mixed + jnp.dot(
                columns, held[row : row + pair_width], preferred_element_type=F32
            )
        return mixed

    def hand_back(outs):
        back = [outs[0]] + [swap_planes(outs[k], k) for k in range(1, PLANES)]
        return jnp.concatenate(back, axis=1)

    mixed = jnp.zeros((rows, out_cols), F32)
    rest = outs = None
    for c in range(len(chunks)):
        own, mine, theirs_now = received[c]
        if c > 0:
            own = after(own, outs)
            near_before = hand_back(outs)
        state = attend(near_flags, own, mine, None, False)
        if c > 0:
            near_before, state = lax.optimization_barrier((near_before, state))
            mixed = project(mixed, near_before, across(near_before), c - 1, part, rest)
        if c + 1 < len(chunks):
            coming = [packed[c + 1][0]] + list(
                after(tuple(packed[c + 1][1:]), own[1], own[2])
            )
            received.append(receive(coming, state, part))
        if rest is None:
            rest = swap(part, 1)
            state = after(state, rest)
        outs = attend(far_flags, own, theirs_now, list(state), True)
    near = hand_back(outs)
    far, mixed = lax.optimization_barrier((across(near), mixed))
    mixed = project(mixed, near, far, len(chunks) - 1, part, rest)
    return mixed.astype(BF16)


def body(query_rows, key_rows, value_rows, pattern, owners, out_weight):
    fits = (
        lax.axis_size("seq") == GROUP * PLANES
        and lax.axis_size("head") == 2
        and (query_rows.shape[1] // HD) % PLANES == 0
    )
    plan = grouped_body if fits else plain_body
    return plan(query_rows, key_rows, value_rows, pattern, owners, out_weight)


def solution(mesh):
    return jax.shard_map(
        body,
        mesh=mesh,
        in_specs=(
            P("seq", "head"),
            P("seq", "head"),
            P("seq", "head"),
            P("seq", None),
            P(),
            P("head", None),
        ),
        out_specs=P("seq", "head"),
        check_vma=False,
    )
```

```python
import functools

import jax
import jax.numpy as jnp
from jax import lax
from jax.experimental import pallas as pl
from jax.experimental.pallas import tpu as pltpu
from jax.sharding import PartitionSpec as P

HD = 128
REACH = 3
OWNERS = 4
REF_DEV = 256
GROUP = 4
PLANES = 4
CHUNKS = (2, 1)
PAT_ROWS = 16
NEG = -1e30
LOG2E = 1.4426950408889634
F32 = jnp.float32
BF16 = jnp.bfloat16


def broadcast(block, axis, owner):
    block = jnp.where(lax.axis_index(axis) == owner, block, jnp.zeros_like(block))
    return lax.psum(block, axis)


def from_behind(value, axis, steps):
    count = lax.axis_size(axis)
    pairs = [(source, (source + steps) % count) for source in range(count)]
    return lax.ppermute(value, axis, pairs)


def column_of(offset):
    return offset + REACH if offset < 0 else offset + REACH - 1


def merge_block(state, query_three, block_keys, block_values):
    peaks, totals, summed_values = state
    local_heads = query_three.shape[1]
    keys_three = block_keys.reshape(-1, local_heads, HD)
    values_three = block_values.reshape(-1, local_heads, HD)
    scores = jnp.einsum(
        "qhd,khd->hqk", query_three, keys_three, preferred_element_type=jnp.float32
    ) * HD ** (-0.5)
    new_peaks = jnp.maximum(peaks, jnp.max(scores, axis=-1))
    rescale = jnp.exp(peaks - new_peaks)
    weights = jnp.exp(scores - new_peaks[:, :, None])
    totals = totals * rescale + jnp.sum(weights, axis=-1)
    contrib = jnp.einsum(
        "hqk,khd->hqd",
        weights.astype(jnp.bfloat16),
        values_three,
        preferred_element_type=jnp.float32,
    )
    summed_values = summed_values * rescale[:, :, None] + contrib
    return (new_peaks, totals, summed_values)


def absorb(state, query_three, stacked, active):
    return lax.cond(
        active,
        lambda inner: merge_block(inner, query_three, stacked[0], stacked[1]),
        lambda inner: inner,
        state,
    )


def plain_body(query_rows, key_rows, value_rows, pattern, owners, out_weight):
    row_count = query_rows.shape[0]
    local_width = query_rows.shape[1]
    local_heads = local_width // HD
    query_three = query_rows.reshape(row_count, local_heads, HD)
    start_state = (
        jnp.full((local_heads, row_count), -jnp.inf, jnp.float32),
        jnp.zeros((local_heads, row_count), jnp.float32),
        jnp.zeros((local_heads, row_count, HD), jnp.float32),
    )
    state = merge_block(start_state, query_three, key_rows, value_rows)
    own_stack = jnp.stack([key_rows, value_rows])
    ref_stack = jnp.stack([key_rows[:REF_DEV], value_rows[:REF_DEV]])
    for member in range(OWNERS):
        arrived = broadcast(ref_stack, "seq", owners[member])
        state = merge_block(state, query_three, arrived[0], arrived[1])
    for distance in range(1, REACH + 1):
        for offset in (-distance, distance):
            arrived = from_behind(own_stack, "seq", -offset)
            state = absorb(state, query_three, arrived, pattern[0, column_of(offset)] != 0)
    peaks, totals, summed_values = state
    attended = summed_values / totals[:, :, None]
    attended = (
        jnp.transpose(attended, (1, 0, 2)).reshape(row_count, local_width).astype(jnp.bfloat16)
    )
    partial_value = jnp.dot(attended, out_weight, preferred_element_type=jnp.float32)
    return lax.psum_scatter(
        partial_value.astype(jnp.bfloat16), "head", scatter_dimension=1, tiled=True
    )


def attend_kernel(heads, plan, first, last, flags_ref, *refs):
    slots = sum(plan)
    q_in = refs[:GROUP]
    ins = refs[GROUP : GROUP + len(plan)]
    rest = refs[GROUP + len(plan) :]
    if not first:
        state_in, rest = rest[:3], rest[3:]
    outs, rest = rest[: GROUP if last else 3], rest[GROUP if last else 3 :]
    q_buf, kv_buf, vt_buf, todo, peak, total, acc, q_sem, kv_sem, state_sem = rest
    rows = q_buf.shape[1]
    width = heads * HD
    scale = HD**-0.5 * LOG2E
    copies = [
        pltpu.make_async_copy(q_in[m].at[2, pl.ds(0, rows)], q_buf.at[m], q_sem.at[m])
        for m in range(GROUP)
    ]
    if first:
        peak[...] = jnp.full(peak.shape, NEG, F32)
        total[...] = jnp.zeros(total.shape, F32)
        acc[...] = jnp.zeros(acc.shape, F32)
    else:
        for n, buf in enumerate((peak, total, acc)):
            copies.append(pltpu.make_async_copy(state_in[n], buf, state_sem.at[n]))
    slot = 0
    for ref, count in zip(ins, plan):
        for j in range(count):
            copies.append(pltpu.make_async_copy(ref.at[j], kv_buf.at[slot], kv_sem.at[slot]))
            slot += 1
    for copy in copies:
        copy.start()

    counts = []
    for m in range(GROUP):

        def note(s, at):
            todo[m, at] = s
            return at + jnp.where(flags_ref[m, s] > 0, 1, 0)

        count = lax.fori_loop(0, slots, note, 0)
        todo[m, count] = -1
        counts.append(count)
    for copy in copies:
        copy.wait()

    def turn(s, _):
        for h in range(heads):
            vt_buf[s, h] = kv_buf[s, 1, :, pl.ds(h * HD, HD)].T
        return 0

    lax.fori_loop(0, slots, turn, 0)
    ends = (0, REF_DEV, rows)

    def one_query(m):
        def pair(p, _):
            chosen = []
            for e in range(2):
                s = todo[m, 2 * p + e]
                shut = s < 0
                s = jnp.maximum(s, 0)
                flag = jnp.where(shut, 0, flags_ref[m, s])
                some = jnp.where(flag == 3, 1.0, jnp.where(flag == 0, NEG, 0.0))
                other = jnp.where((flag & 1) == 1, 0.0, NEG)
                chosen.append((s, (some, other)))
            for h in range(heads):
                cols = pl.ds(h * HD, HD)
                q = q_buf[m, :, cols]
                new = peak[m, h]
                scores = []
                for s, bias in chosen:
                    for part in range(2):
                        k = kv_buf[s, 0, pl.ds(ends[part], ends[part + 1] - ends[part]), cols]
                        raw = (
                            lax.dot_general(
                                k, q, (((1,), (1,)), ((), ())), preferred_element_type=F32
                            )
                            * scale
                        )
                        new = jnp.maximum(new, jnp.max(raw, axis=0, keepdims=True) + bias[part])
                        scores.append((raw, bias[part]))
                keep = jnp.exp2(peak[m, h] - new)
                sums = total[m, h] * keep
                out = acc[m, h] * keep
                for e, (s, _) in enumerate(chosen):
                    weights = []
                    for raw, bias in scores[2 * e : 2 * e + 2]:
                        weight = jnp.exp2(raw - (new - bias))
                        sums = sums + jnp.sum(weight, axis=0, keepdims=True)
                        weights.append(weight.astype(BF16))
                    out = out + jnp.dot(
                        vt_buf[s, h], jnp.concatenate(weights, axis=0), preferred_element_type=F32
                    )
                peak[m, h] = new
                total[m, h] = sums
                acc[m, h] = out
            return 0

        lax.fori_loop(0, (counts[m] + 1) // 2, pair, 0)

    for m in range(GROUP):
        one_query(m)
    if last:
        for m in range(GROUP):
            for h in range(heads):
                outs[m][:, pl.ds(h * HD, HD)] = (acc[m, h] / total[m, h]).T.astype(BF16)
    else:
        for out, buf in zip(outs, (peak, total, acc)):
            out[...] = buf[...]


def attend(flags, own, held, state, last):
    rows, width = held[0].shape[2:]
    heads = width // HD
    plan = tuple(array.shape[0] for array in held)
    slots = sum(plan)
    any_spec = pl.BlockSpec(memory_space=pl.ANY)
    vmem_spec = pl.BlockSpec(memory_space=pltpu.VMEM)
    state_shapes = [(GROUP, heads, 1, rows)] * 2 + [(GROUP, heads, HD, rows)]
    if last:
        out_shape = [jax.ShapeDtypeStruct((rows, width), BF16)] * GROUP
    else:
        out_shape = [jax.ShapeDtypeStruct(shape, F32) for shape in state_shapes]
    state = state or []
    return pl.pallas_call(
        functools.partial(attend_kernel, heads, plan, not state, last),
        out_shape=out_shape,
        in_specs=[pl.BlockSpec(memory_space=pltpu.SMEM)]
        + [any_spec] * (GROUP + len(held) + len(state)),
        out_specs=[vmem_spec] * len(out_shape),
        scratch_shapes=[
            pltpu.VMEM((GROUP, rows, width), BF16),
            pltpu.VMEM((slots, 2, rows, width), BF16),
            pltpu.VMEM((slots, heads, HD, rows), BF16),
            pltpu.SMEM((GROUP, slots + 2), jnp.int32),
        ]
        + [pltpu.VMEM(shape, F32) for shape in state_shapes]
        + [
            pltpu.SemaphoreType.DMA((GROUP,)),
            pltpu.SemaphoreType.DMA((slots,)),
            pltpu.SemaphoreType.DMA((3,)),
        ],
        compiler_params=pltpu.CompilerParams(vmem_limit_bytes=20 << 20),
        cost_estimate=pl.CostEstimate(flops=0, bytes_accessed=0, transcendentals=0),
        name="attend_slots",
    )(flags, *own, *held, *state)


def grouped_body(query_rows, key_rows, value_rows, pattern, owners, out_weight):
    rows, width = query_rows.shape
    out_cols = out_weight.shape[1] // 2
    blocks = GROUP * PLANES
    index = lax.axis_index("seq")
    side = lax.axis_index("head")
    plane, member = index // GROUP, index % GROUP
    per_plane = width // HD // PLANES
    chunks = CHUNKS if sum(CHUNKS) == per_plane else (per_plane,)
    starts = [sum(chunks[:c]) for c in range(len(chunks))]

    def swap(value, bits):
        return lax.ppermute(value, "seq", [(i, i ^ bits) for i in range(blocks)])

    def swap_planes(value, k):
        return swap(value, GROUP * k)

    def across(value):
        return lax.ppermute(value, "head", [(0, 1), (1, 0)])

    def after(value, *others):
        return lax.optimization_barrier((value, others))[0]

    def stack(pieces):
        return jnp.stack([piece[:2, :rows] for piece in pieces])

    def pack_heads(arrays, start, heads):
        note = jnp.pad(
            (pattern != 0).astype(BF16)[None],
            ((0, 2), (rows, PAT_ROWS - 1), (0, heads * HD - 2 * REACH)),
        )
        pieces = []
        for k in range(PLANES):
            first = ((plane ^ k) * per_plane + start) * HD
            piece = jnp.stack(
                [lax.dynamic_slice_in_dim(array, first, heads * HD, 1) for array in arrays]
            )
            pieces.append(jnp.pad(piece, ((0, 0), (0, PAT_ROWS), (0, 0))) + note)
        return pieces

    arrays = (key_rows, value_rows, query_rows)
    half = width // 2
    core = index % 2
    packed = [pack_heads(arrays, starts[0], chunks[0])]

    def weight_rows(weight, side_at, away, c):
        return [
            lax.dynamic_slice(
                weight,
                (((plane ^ k) * per_plane + starts[c]) * HD, side_at * out_cols),
                (chunks[c] * HD, out_cols),
            )
            for k in away
        ]

    weight = after(out_weight, packed[0])
    weight_sides = [
        [
            jnp.concatenate(weight_rows(weight, at, range(PLANES), c))
            for c in range(len(chunks))
        ]
        for at in (side, 1 - side)
    ]
    final = len(chunks) - 1
    part = across(
        jnp.concatenate(weight_rows(weight, 1 - side, (2 * core, 2 * core + 1), final))
    )
    rest = swap(part, 1)
    for c in range(1, len(chunks)):
        arrays = after(arrays, packed[-1])
        packed.append(pack_heads(arrays, starts[c], chunks[c]))

    def receive(pieces, *gate):
        pieces = [pieces[0]] + [swap_planes(pieces[k], k) for k in range(1, PLANES)]
        if gate:
            pieces[1:] = after(pieces[1:], *gate)
        low = stack(pieces[:2])
        chip_low = swap(low, 2)
        if not gate:
            pieces[2:] = after(pieces[2:], chip_low, weight_sides, rest)
        high = stack(pieces[2:])
        chip_high = swap(high, 2)
        mine = [low, high, swap(low, 1), swap(high, 1)]
        return pieces, mine, [chip_low, chip_high, swap(chip_low, 1), swap(chip_high, 1)]

    received = [receive(packed[0])]

    planes_at = (plane ^ jnp.arange(PLANES, dtype=jnp.int32)) * GROUP
    my_blocks = planes_at + member
    held = jnp.concatenate([planes_at + (member ^ m) for m in range(GROUP)])
    my_pattern = jnp.stack([piece[0, rows, : 2 * REACH] for piece in received[0][0]])
    away = (held[None, :] - my_blocks[:, None]) % blocks
    full = (away == 0).astype(jnp.int32)
    for offset in list(range(-REACH, 0)) + list(range(1, REACH + 1)):
        chosen = (my_pattern[:, column_of(offset)] != 0)[:, None]
        full = full + (chosen & (away == offset % blocks)).astype(jnp.int32)
    is_ref = jnp.any(held[:, None] == owners[None, :], axis=1).astype(jnp.int32)
    flags = full + 2 * is_ref[None, :]
    near_flags, far_flags = flags[:, : 2 * PLANES], flags[:, 2 * PLANES :]

    def project(total, near, at, c):
        return total + jnp.dot(near, weight_sides[at][c], preferred_element_type=F32)

    def hand_back(outs):
        back = [outs[0]] + [swap_planes(outs[k], k) for k in range(1, PLANES)]
        return jnp.concatenate(back, axis=1)

    kept = given = jnp.zeros((rows, out_cols), F32)
    outs = None
    for c in range(len(chunks)):
        own, mine, theirs_now = received[c]
        if c > 0:
            own = after(own, outs)
            near_before = hand_back(outs)
        state = attend(near_flags, own, mine, None, False)
        if c > 0:
            near_before, state = lax.optimization_barrier((near_before, state))
            kept = project(kept, near_before, 0, c - 1)
            given = project(given, near_before, 1, c - 1)
        if c + 1 < len(chunks):
            coming = [packed[c + 1][0]] + list(
                after(tuple(packed[c + 1][1:]), own[1], own[2])
            )
            received.append(receive(coming, state))
            state = after(state, received[-1][1][0])
        outs = attend(far_flags, own, theirs_now, list(state), True)
    near = hand_back(outs)
    far = across(near)
    mixed = project(kept, near, 0, final)
    if final > 0:
        taken = across(given.astype(BF16))
        mixed = mixed + taken.astype(F32)
    far, mixed = lax.optimization_barrier((far, mixed))
    pair_width = far.shape[1] // 2
    for at, held_rows in ((core, part), (1 - core, rest)):
        columns = lax.dynamic_slice_in_dim(far, at * pair_width, pair_width, 1)
        mixed = mixed + jnp.dot(columns, held_rows, preferred_element_type=F32)
    return mixed.astype(BF16)


def body(query_rows, key_rows, value_rows, pattern, owners, out_weight):
    fits = (
        lax.axis_size("seq") == GROUP * PLANES
        and lax.axis_size("head") == 2
        and (query_rows.shape[1] // HD) % PLANES == 0
    )
    plan = grouped_body if fits else plain_body
    return plan(query_rows, key_rows, value_rows, pattern, owners, out_weight)


def solution(mesh):
    return jax.shard_map(
        body,
        mesh=mesh,
        in_specs=(
            P("seq", "head"),
            P("seq", "head"),
            P("seq", "head"),
            P("seq", None),
            P(),
            P("head", None),
        ),
        out_specs=P("seq", "head"),
        check_vma=False,
    )
```

```python
import functools

import jax
import jax.numpy as jnp
from jax import lax
from jax.experimental import pallas as pl
from jax.experimental.pallas import tpu as pltpu
from jax.sharding import PartitionSpec as P

HD = 128
REACH = 3
OWNERS = 4
REF_DEV = 256
GROUP = 4
PLANES = 4
CHUNKS = (2, 1)
PAT_ROWS = 16
NEG = -1e30
LOG2E = 1.4426950408889634
F32 = jnp.float32
BF16 = jnp.bfloat16


def broadcast(block, axis, owner):
    block = jnp.where(lax.axis_index(axis) == owner, block, jnp.zeros_like(block))
    return lax.psum(block, axis)


def from_behind(value, axis, steps):
    count = lax.axis_size(axis)
    pairs = [(source, (source + steps) % count) for source in range(count)]
    return lax.ppermute(value, axis, pairs)


def column_of(offset):
    return offset + REACH if offset < 0 else offset + REACH - 1


def merge_block(state, query_three, block_keys, block_values):
    peaks, totals, summed_values = state
    local_heads = query_three.shape[1]
    keys_three = block_keys.reshape(-1, local_heads, HD)
    values_three = block_values.reshape(-1, local_heads, HD)
    scores = jnp.einsum(
        "qhd,khd->hqk", query_three, keys_three, preferred_element_type=jnp.float32
    ) * HD ** (-0.5)
    new_peaks = jnp.maximum(peaks, jnp.max(scores, axis=-1))
    rescale = jnp.exp(peaks - new_peaks)
    weights = jnp.exp(scores - new_peaks[:, :, None])
    totals = totals * rescale + jnp.sum(weights, axis=-1)
    contrib = jnp.einsum(
        "hqk,khd->hqd",
        weights.astype(jnp.bfloat16),
        values_three,
        preferred_element_type=jnp.float32,
    )
    summed_values = summed_values * rescale[:, :, None] + contrib
    return (new_peaks, totals, summed_values)


def absorb(state, query_three, stacked, active):
    return lax.cond(
        active,
        lambda inner: merge_block(inner, query_three, stacked[0], stacked[1]),
        lambda inner: inner,
        state,
    )


def plain_body(query_rows, key_rows, value_rows, pattern, owners, out_weight):
    row_count = query_rows.shape[0]
    local_width = query_rows.shape[1]
    local_heads = local_width // HD
    query_three = query_rows.reshape(row_count, local_heads, HD)
    start_state = (
        jnp.full((local_heads, row_count), -jnp.inf, jnp.float32),
        jnp.zeros((local_heads, row_count), jnp.float32),
        jnp.zeros((local_heads, row_count, HD), jnp.float32),
    )
    state = merge_block(start_state, query_three, key_rows, value_rows)
    own_stack = jnp.stack([key_rows, value_rows])
    ref_stack = jnp.stack([key_rows[:REF_DEV], value_rows[:REF_DEV]])
    for member in range(OWNERS):
        arrived = broadcast(ref_stack, "seq", owners[member])
        state = merge_block(state, query_three, arrived[0], arrived[1])
    for distance in range(1, REACH + 1):
        for offset in (-distance, distance):
            arrived = from_behind(own_stack, "seq", -offset)
            state = absorb(state, query_three, arrived, pattern[0, column_of(offset)] != 0)
    peaks, totals, summed_values = state
    attended = summed_values / totals[:, :, None]
    attended = (
        jnp.transpose(attended, (1, 0, 2)).reshape(row_count, local_width).astype(jnp.bfloat16)
    )
    partial_value = jnp.dot(attended, out_weight, preferred_element_type=jnp.float32)
    return lax.psum_scatter(
        partial_value.astype(jnp.bfloat16), "head", scatter_dimension=1, tiled=True
    )


def attend_kernel(heads, plan, first, last, flags_ref, *refs):
    slots = sum(plan)
    q_in = refs[:GROUP]
    ins = refs[GROUP : GROUP + len(plan)]
    rest = refs[GROUP + len(plan) :]
    if not first:
        state_in, rest = rest[:3], rest[3:]
    outs, rest = rest[: GROUP if last else 3], rest[GROUP if last else 3 :]
    q_buf, kv_buf, vt_buf, todo, peak, total, acc, q_sem, kv_sem, state_sem = rest
    rows = q_buf.shape[1]
    width = heads * HD
    scale = HD**-0.5 * LOG2E
    copies = [
        pltpu.make_async_copy(q_in[m].at[2, pl.ds(0, rows)], q_buf.at[m], q_sem.at[m])
        for m in range(GROUP)
    ]
    if first:
        peak[...] = jnp.full(peak.shape, NEG, F32)
        total[...] = jnp.zeros(total.shape, F32)
        acc[...] = jnp.zeros(acc.shape, F32)
    else:
        for n, buf in enumerate((peak, total, acc)):
            copies.append(pltpu.make_async_copy(state_in[n], buf, state_sem.at[n]))
    slot = 0
    for ref, count in zip(ins, plan):
        for j in range(count):
            copies.append(pltpu.make_async_copy(ref.at[j], kv_buf.at[slot], kv_sem.at[slot]))
            slot += 1
    for copy in copies:
        copy.start()

    counts = []
    for m in range(GROUP):

        def note(s, at):
            todo[m, at] = s
            return at + jnp.where(flags_ref[m, s] > 0, 1, 0)

        count = lax.fori_loop(0, slots, note, 0)
        todo[m, count] = -1
        counts.append(count)
    for copy in copies:
        copy.wait()

    def turn(s, _):
        for h in range(heads):
            vt_buf[s, h] = kv_buf[s, 1, :, pl.ds(h * HD, HD)].T
        return 0

    lax.fori_loop(0, slots, turn, 0)
    ends = (0, REF_DEV, rows)

    def one_query(m):
        def pair(p, _):
            chosen = []
            for e in range(2):
                s = todo[m, 2 * p + e]
                shut = s < 0
                s = jnp.maximum(s, 0)
                flag = jnp.where(shut, 0, flags_ref[m, s])
                some = jnp.where(flag == 3, 1.0, jnp.where(flag == 0, NEG, 0.0))
                other = jnp.where((flag & 1) == 1, 0.0, NEG)
                chosen.append((s, (some, other)))
            for h in range(heads):
                cols = pl.ds(h * HD, HD)
                q = q_buf[m, :, cols]
                new = peak[m, h]
                scores = []
                for s, bias in chosen:
                    for part in range(2):
                        k = kv_buf[s, 0, pl.ds(ends[part], ends[part + 1] - ends[part]), cols]
                        raw = (
                            lax.dot_general(
                                k, q, (((1,), (1,)), ((), ())), preferred_element_type=F32
                            )
                            * scale
                        )
                        new = jnp.maximum(new, jnp.max(raw, axis=0, keepdims=True) + bias[part])
                        scores.append((raw, bias[part]))
                keep = jnp.exp2(peak[m, h] - new)
                sums = total[m, h] * keep
                out = acc[m, h] * keep
                for e, (s, _) in enumerate(chosen):
                    weights = []
                    for raw, bias in scores[2 * e : 2 * e + 2]:
                        weight = jnp.exp2(raw - (new - bias))
                        sums = sums + jnp.sum(weight, axis=0, keepdims=True)
                        weights.append(weight.astype(BF16))
                    out = out + jnp.dot(
                        vt_buf[s, h], jnp.concatenate(weights, axis=0), preferred_element_type=F32
                    )
                peak[m, h] = new
                total[m, h] = sums
                acc[m, h] = out
            return 0

        lax.fori_loop(0, (counts[m] + 1) // 2, pair, 0)

    for m in range(GROUP):
        one_query(m)
    if last:
        for m in range(GROUP):
            for h in range(heads):
                outs[m][:, pl.ds(h * HD, HD)] = (acc[m, h] / total[m, h]).T.astype(BF16)
    else:
        for out, buf in zip(outs, (peak, total, acc)):
            out[...] = buf[...]


def attend(flags, own, held, state, last):
    rows, width = held[0].shape[2:]
    heads = width // HD
    plan = tuple(array.shape[0] for array in held)
    slots = sum(plan)
    any_spec = pl.BlockSpec(memory_space=pl.ANY)
    vmem_spec = pl.BlockSpec(memory_space=pltpu.VMEM)
    state_shapes = [(GROUP, heads, 1, rows)] * 2 + [(GROUP, heads, HD, rows)]
    if last:
        out_shape = [jax.ShapeDtypeStruct((rows, width), BF16)] * GROUP
    else:
        out_shape = [jax.ShapeDtypeStruct(shape, F32) for shape in state_shapes]
    state = state or []
    return pl.pallas_call(
        functools.partial(attend_kernel, heads, plan, not state, last),
        out_shape=out_shape,
        in_specs=[pl.BlockSpec(memory_space=pltpu.SMEM)]
        + [any_spec] * (GROUP + len(held) + len(state)),
        out_specs=[vmem_spec] * len(out_shape),
        scratch_shapes=[
            pltpu.VMEM((GROUP, rows, width), BF16),
            pltpu.VMEM((slots, 2, rows, width), BF16),
            pltpu.VMEM((slots, heads, HD, rows), BF16),
            pltpu.SMEM((GROUP, slots + 2), jnp.int32),
        ]
        + [pltpu.VMEM(shape, F32) for shape in state_shapes]
        + [
            pltpu.SemaphoreType.DMA((GROUP,)),
            pltpu.SemaphoreType.DMA((slots,)),
            pltpu.SemaphoreType.DMA((3,)),
        ],
        compiler_params=pltpu.CompilerParams(vmem_limit_bytes=20 << 20),
        cost_estimate=pl.CostEstimate(flops=0, bytes_accessed=0, transcendentals=0),
        name="attend_slots",
    )(flags, *own, *held, *state)


def grouped_body(query_rows, key_rows, value_rows, pattern, owners, out_weight):
    rows, width = query_rows.shape
    out_cols = out_weight.shape[1] // 2
    blocks = GROUP * PLANES
    index = lax.axis_index("seq")
    side = lax.axis_index("head")
    plane, member = index // GROUP, index % GROUP
    per_plane = width // HD // PLANES
    chunks = CHUNKS if sum(CHUNKS) == per_plane else (per_plane,)
    starts = [sum(chunks[:c]) for c in range(len(chunks))]

    def swap(value, bits):
        return lax.ppermute(value, "seq", [(i, i ^ bits) for i in range(blocks)])

    def swap_planes(value, k):
        return swap(value, GROUP * k)

    def across(value):
        return lax.ppermute(value, "head", [(0, 1), (1, 0)])

    def after(value, *others):
        return lax.optimization_barrier((value, others))[0]

    def stack(pieces):
        return jnp.stack([piece[:2, :rows] for piece in pieces])

    def pack_heads(arrays, start, heads):
        note = jnp.pad(
            (pattern != 0).astype(BF16)[None],
            ((0, 2), (rows, PAT_ROWS - 1), (0, heads * HD - 2 * REACH)),
        )
        pieces = []
        for k in (1, 2, 3, 0):
            if k == 2:
                arrays = after(arrays, pieces)
            first = ((plane ^ k) * per_plane + start) * HD
            piece = jnp.stack(
                [lax.dynamic_slice_in_dim(array, first, heads * HD, 1) for array in arrays]
            )
            pieces.append(jnp.pad(piece, ((0, 0), (0, PAT_ROWS), (0, 0))) + note)
        return [pieces[3]] + pieces[:3]

    arrays = (key_rows, value_rows, query_rows)
    half = width // 2
    core = index % 2
    packed = [pack_heads(arrays, starts[0], chunks[0])]

    def weight_rows(weight, side_at, away, c):
        return [
            lax.dynamic_slice(
                weight,
                (((plane ^ k) * per_plane + starts[c]) * HD, side_at * out_cols),
                (chunks[c] * HD, out_cols),
            )
            for k in away
        ]

    weight = after(out_weight, packed[0])
    weight_sides = [
        [
            jnp.concatenate(weight_rows(weight, at, range(PLANES), c))
            for c in range(len(chunks))
        ]
        for at in (side, 1 - side)
    ]
    final = len(chunks) - 1
    part = across(
        jnp.concatenate(weight_rows(weight, 1 - side, (2 * core, 2 * core + 1), final))
    )
    rest = swap(part, 1)
    for c in range(1, len(chunks)):
        arrays = after(arrays, packed[-1])
        packed.append(pack_heads(arrays, starts[c], chunks[c]))

    def receive(pieces, *gate):
        pieces = [pieces[0]] + [swap_planes(pieces[k], k) for k in range(1, PLANES)]
        if gate:
            pieces[1:] = after(pieces[1:], *gate)
        low = stack(pieces[:2])
        chip_low = swap(low, 2)
        if not gate:
            pieces[2:] = after(pieces[2:], chip_low, weight_sides, rest)
        high = stack(pieces[2:])
        chip_high = swap(high, 2)
        mine = [low, high, swap(low, 1), swap(high, 1)]
        return pieces, mine, [chip_low, chip_high, swap(chip_low, 1), swap(chip_high, 1)]

    received = [receive(packed[0])]

    planes_at = (plane ^ jnp.arange(PLANES, dtype=jnp.int32)) * GROUP
    my_blocks = planes_at + member
    held = jnp.concatenate([planes_at + (member ^ m) for m in range(GROUP)])
    my_pattern = jnp.stack([piece[0, rows, : 2 * REACH] for piece in received[0][0]])
    away = (held[None, :] - my_blocks[:, None]) % blocks
    full = (away == 0).astype(jnp.int32)
    for offset in list(range(-REACH, 0)) + list(range(1, REACH + 1)):
        chosen = (my_pattern[:, column_of(offset)] != 0)[:, None]
        full = full + (chosen & (away == offset % blocks)).astype(jnp.int32)
    is_ref = jnp.any(held[:, None] == owners[None, :], axis=1).astype(jnp.int32)
    flags = full + 2 * is_ref[None, :]
    near_flags, far_flags = flags[:, : 2 * PLANES], flags[:, 2 * PLANES :]

    def project(total, near, at, c):
        return total + jnp.dot(near, weight_sides[at][c], preferred_element_type=F32)

    def hand_back(outs):
        back = [outs[0]] + [swap_planes(outs[k], k) for k in range(1, PLANES)]
        return jnp.concatenate(back, axis=1)

    kept = given = jnp.zeros((rows, out_cols), F32)
    outs = None
    for c in range(len(chunks)):
        own, mine, theirs_now = received[c]
        if c > 0:
            own = after(own, outs)
            near_before = hand_back(outs)
        state = attend(near_flags, own, mine, None, False)
        if c > 0:
            near_before, state = lax.optimization_barrier((near_before, state))
            kept = project(kept, near_before, 0, c - 1)
            given = project(given, near_before, 1, c - 1)
        if c + 1 < len(chunks):
            coming = [packed[c + 1][0]] + list(
                after(tuple(packed[c + 1][1:]), own[1], own[2])
            )
            received.append(receive(coming, state))
            state = after(state, received[-1][1][0])
        outs = attend(far_flags, own, theirs_now, list(state), True)
    near = hand_back(outs)
    far = across(near)
    mixed = project(kept, near, 0, final)
    if final > 0:
        taken = across(given.astype(BF16))
        mixed = mixed + taken.astype(F32)
    far, mixed = lax.optimization_barrier((far, mixed))
    pair_width = far.shape[1] // 2
    for at, held_rows in ((core, part), (1 - core, rest)):
        columns = lax.dynamic_slice_in_dim(far, at * pair_width, pair_width, 1)
        mixed = mixed + jnp.dot(columns, held_rows, preferred_element_type=F32)
    return mixed.astype(BF16)


def body(query_rows, key_rows, value_rows, pattern, owners, out_weight):
    fits = (
        lax.axis_size("seq") == GROUP * PLANES
        and lax.axis_size("head") == 2
        and (query_rows.shape[1] // HD) % PLANES == 0
    )
    plan = grouped_body if fits else plain_body
    return plan(query_rows, key_rows, value_rows, pattern, owners, out_weight)


def solution(mesh):
    return jax.shard_map(
        body,
        mesh=mesh,
        in_specs=(
            P("seq", "head"),
            P("seq", "head"),
            P("seq", "head"),
            P("seq", None),
            P(),
            P("head", None),
        ),
        out_specs=P("seq", "head"),
        check_vma=False,
    )
```

```python
import functools

import jax
import jax.numpy as jnp
from jax import lax
from jax.experimental import pallas as pl
from jax.experimental.pallas import tpu as pltpu
from jax.sharding import PartitionSpec as P

HD = 128
REACH = 3
OWNERS = 4
REF_DEV = 256
GROUP = 4
PLANES = 4
CHUNKS = (2, 1)
PAT_ROWS = 16
NEG = -1e30
LOG2E = 1.4426950408889634
F32 = jnp.float32
BF16 = jnp.bfloat16


def broadcast(block, axis, owner):
    block = jnp.where(lax.axis_index(axis) == owner, block, jnp.zeros_like(block))
    return lax.psum(block, axis)


def from_behind(value, axis, steps):
    count = lax.axis_size(axis)
    pairs = [(source, (source + steps) % count) for source in range(count)]
    return lax.ppermute(value, axis, pairs)


def column_of(offset):
    return offset + REACH if offset < 0 else offset + REACH - 1


def merge_block(state, query_three, block_keys, block_values):
    peaks, totals, summed_values = state
    local_heads = query_three.shape[1]
    keys_three = block_keys.reshape(-1, local_heads, HD)
    values_three = block_values.reshape(-1, local_heads, HD)
    scores = jnp.einsum(
        "qhd,khd->hqk", query_three, keys_three, preferred_element_type=jnp.float32
    ) * HD ** (-0.5)
    new_peaks = jnp.maximum(peaks, jnp.max(scores, axis=-1))
    rescale = jnp.exp(peaks - new_peaks)
    weights = jnp.exp(scores - new_peaks[:, :, None])
    totals = totals * rescale + jnp.sum(weights, axis=-1)
    contrib = jnp.einsum(
        "hqk,khd->hqd",
        weights.astype(jnp.bfloat16),
        values_three,
        preferred_element_type=jnp.float32,
    )
    summed_values = summed_values * rescale[:, :, None] + contrib
    return (new_peaks, totals, summed_values)


def absorb(state, query_three, stacked, active):
    return lax.cond(
        active,
        lambda inner: merge_block(inner, query_three, stacked[0], stacked[1]),
        lambda inner: inner,
        state,
    )


def plain_body(query_rows, key_rows, value_rows, pattern, owners, out_weight):
    row_count = query_rows.shape[0]
    local_width = query_rows.shape[1]
    local_heads = local_width // HD
    query_three = query_rows.reshape(row_count, local_heads, HD)
    start_state = (
        jnp.full((local_heads, row_count), -jnp.inf, jnp.float32),
        jnp.zeros((local_heads, row_count), jnp.float32),
        jnp.zeros((local_heads, row_count, HD), jnp.float32),
    )
    state = merge_block(start_state, query_three, key_rows, value_rows)
    own_stack = jnp.stack([key_rows, value_rows])
    ref_stack = jnp.stack([key_rows[:REF_DEV], value_rows[:REF_DEV]])
    for member in range(OWNERS):
        arrived = broadcast(ref_stack, "seq", owners[member])
        state = merge_block(state, query_three, arrived[0], arrived[1])
    for distance in range(1, REACH + 1):
        for offset in (-distance, distance):
            arrived = from_behind(own_stack, "seq", -offset)
            state = absorb(state, query_three, arrived, pattern[0, column_of(offset)] != 0)
    peaks, totals, summed_values = state
    attended = summed_values / totals[:, :, None]
    attended = (
        jnp.transpose(attended, (1, 0, 2)).reshape(row_count, local_width).astype(jnp.bfloat16)
    )
    partial_value = jnp.dot(attended, out_weight, preferred_element_type=jnp.float32)
    return lax.psum_scatter(
        partial_value.astype(jnp.bfloat16), "head", scatter_dimension=1, tiled=True
    )


def attend_kernel(heads, plan, first, last, flags_ref, *refs):
    slots = sum(plan)
    q_in = refs[:GROUP]
    ins = refs[GROUP : GROUP + len(plan)]
    rest = refs[GROUP + len(plan) :]
    if not first:
        state_in, rest = rest[:3], rest[3:]
    outs, rest = rest[: GROUP if last else 3], rest[GROUP if last else 3 :]
    q_buf, kv_buf, vt_buf, todo, peak, total, acc, q_sem, kv_sem, state_sem = rest
    rows = q_buf.shape[1]
    width = heads * HD
    scale = HD**-0.5 * LOG2E
    copies = [
        pltpu.make_async_copy(q_in[m].at[2, pl.ds(0, rows)], q_buf.at[m], q_sem.at[m])
        for m in range(GROUP)
    ]
    if first:
        peak[...] = jnp.full(peak.shape, NEG, F32)
        total[...] = jnp.zeros(total.shape, F32)
        acc[...] = jnp.zeros(acc.shape, F32)
    else:
        for n, buf in enumerate((peak, total, acc)):
            copies.append(pltpu.make_async_copy(state_in[n], buf, state_sem.at[n]))
    slot = 0
    for ref, count in zip(ins, plan):
        for j in range(count):
            copies.append(pltpu.make_async_copy(ref.at[j], kv_buf.at[slot], kv_sem.at[slot]))
            slot += 1
    for copy in copies:
        copy.start()

    counts = []
    for m in range(GROUP):

        def note(s, at):
            todo[m, at] = s
            return at + jnp.where(flags_ref[m, s] > 0, 1, 0)

        count = lax.fori_loop(0, slots, note, 0)
        todo[m, count] = -1
        counts.append(count)
    for copy in copies:
        copy.wait()

    def turn(s, _):
        for h in range(heads):
            vt_buf[s, h] = kv_buf[s, 1, :, pl.ds(h * HD, HD)].T
        return 0

    lax.fori_loop(0, slots, turn, 0)
    ends = (0, REF_DEV, rows)

    def one_query(m):
        def pair(p, _):
            chosen = []
            for e in range(2):
                s = todo[m, 2 * p + e]
                shut = s < 0
                s = jnp.maximum(s, 0)
                flag = jnp.where(shut, 0, flags_ref[m, s])
                some = jnp.where(flag == 3, 1.0, jnp.where(flag == 0, NEG, 0.0))
                other = jnp.where((flag & 1) == 1, 0.0, NEG)
                chosen.append((s, (some, other)))
            for h in range(heads):
                cols = pl.ds(h * HD, HD)
                q = q_buf[m, :, cols]
                new = peak[m, h]
                scores = []
                for s, bias in chosen:
                    for part in range(2):
                        k = kv_buf[s, 0, pl.ds(ends[part], ends[part + 1] - ends[part]), cols]
                        raw = (
                            lax.dot_general(
                                k, q, (((1,), (1,)), ((), ())), preferred_element_type=F32
                            )
                            * scale
                        )
                        new = jnp.maximum(new, jnp.max(raw, axis=0, keepdims=True) + bias[part])
                        scores.append((raw, bias[part]))
                keep = jnp.exp2(peak[m, h] - new)
                sums = total[m, h] * keep
                out = acc[m, h] * keep
                for e, (s, _) in enumerate(chosen):
                    weights = []
                    for raw, bias in scores[2 * e : 2 * e + 2]:
                        weight = jnp.exp2(raw - (new - bias))
                        sums = sums + jnp.sum(weight, axis=0, keepdims=True)
                        weights.append(weight.astype(BF16))
                    out = out + jnp.dot(
                        vt_buf[s, h], jnp.concatenate(weights, axis=0), preferred_element_type=F32
                    )
                peak[m, h] = new
                total[m, h] = sums
                acc[m, h] = out
            return 0

        lax.fori_loop(0, (counts[m] + 1) // 2, pair, 0)

    for m in range(GROUP):
        one_query(m)
    if last:
        for m in range(GROUP):
            for h in range(heads):
                outs[m][:, pl.ds(h * HD, HD)] = (acc[m, h] / total[m, h]).T.astype(BF16)
    else:
        for out, buf in zip(outs, (peak, total, acc)):
            out[...] = buf[...]


def attend(flags, own, held, state, last):
    rows, width = held[0].shape[2:]
    heads = width // HD
    plan = tuple(array.shape[0] for array in held)
    slots = sum(plan)
    any_spec = pl.BlockSpec(memory_space=pl.ANY)
    vmem_spec = pl.BlockSpec(memory_space=pltpu.VMEM)
    state_shapes = [(GROUP, heads, 1, rows)] * 2 + [(GROUP, heads, HD, rows)]
    if last:
        out_shape = [jax.ShapeDtypeStruct((rows, width), BF16)] * GROUP
    else:
        out_shape = [jax.ShapeDtypeStruct(shape, F32) for shape in state_shapes]
    state = state or []
    return pl.pallas_call(
        functools.partial(attend_kernel, heads, plan, not state, last),
        out_shape=out_shape,
        in_specs=[pl.BlockSpec(memory_space=pltpu.SMEM)]
        + [any_spec] * (GROUP + len(held) + len(state)),
        out_specs=[vmem_spec] * len(out_shape),
        scratch_shapes=[
            pltpu.VMEM((GROUP, rows, width), BF16),
            pltpu.VMEM((slots, 2, rows, width), BF16),
            pltpu.VMEM((slots, heads, HD, rows), BF16),
            pltpu.SMEM((GROUP, slots + 2), jnp.int32),
        ]
        + [pltpu.VMEM(shape, F32) for shape in state_shapes]
        + [
            pltpu.SemaphoreType.DMA((GROUP,)),
            pltpu.SemaphoreType.DMA((slots,)),
            pltpu.SemaphoreType.DMA((3,)),
        ],
        compiler_params=pltpu.CompilerParams(vmem_limit_bytes=20 << 20),
        cost_estimate=pl.CostEstimate(flops=0, bytes_accessed=0, transcendentals=0),
        name="attend_slots",
    )(flags, *own, *held, *state)


def grouped_body(query_rows, key_rows, value_rows, pattern, owners, out_weight):
    rows, width = query_rows.shape
    out_cols = out_weight.shape[1] // 2
    blocks = GROUP * PLANES
    index = lax.axis_index("seq")
    side = lax.axis_index("head")
    plane, member = index // GROUP, index % GROUP
    per_plane = width // HD // PLANES
    chunks = CHUNKS if sum(CHUNKS) == per_plane else (per_plane,)
    starts = [sum(chunks[:c]) for c in range(len(chunks))]

    def swap(value, bits):
        return lax.ppermute(value, "seq", [(i, i ^ bits) for i in range(blocks)])

    def swap_planes(value, k):
        return swap(value, GROUP * k)

    def across(value):
        return lax.ppermute(value, "head", [(0, 1), (1, 0)])

    def after(value, *others):
        return lax.optimization_barrier((value, others))[0]

    def stack(pieces):
        return jnp.stack([piece[:2, :rows] for piece in pieces])

    def pack_heads(arrays, start, heads):
        note = jnp.pad(
            (pattern != 0).astype(BF16)[None],
            ((0, 2), (rows, PAT_ROWS - 1), (0, heads * HD - 2 * REACH)),
        )
        pieces = []
        for k in (1, 2, 3, 0):
            if k == 2:
                arrays = after(arrays, pieces)
            first = ((plane ^ k) * per_plane + start) * HD
            piece = jnp.stack(
                [lax.dynamic_slice_in_dim(array, first, heads * HD, 1) for array in arrays]
            )
            pieces.append(jnp.pad(piece, ((0, 0), (0, PAT_ROWS), (0, 0))) + note)
        return [pieces[3]] + pieces[:3]

    arrays = (key_rows, value_rows, query_rows)
    half = width // 2
    core = index % 2
    packed = [pack_heads(arrays, starts[0], chunks[0])]

    def weight_rows(weight, side_at, away, c):
        return [
            lax.dynamic_slice(
                weight,
                (((plane ^ k) * per_plane + starts[c]) * HD, side_at * out_cols),
                (chunks[c] * HD, out_cols),
            )
            for k in away
        ]

    weight = after(out_weight, packed[0])
    weight_sides = [
        [
            jnp.concatenate(weight_rows(weight, at, range(PLANES), c))
            for c in range(len(chunks))
        ]
        for at in (side, 1 - side)
    ]
    final = len(chunks) - 1
    part = across(
        jnp.concatenate(weight_rows(weight, 1 - side, (2 * core, 2 * core + 1), final))
    )
    far_rows = jnp.concatenate([part, swap(part, 1)])
    for c in range(1, len(chunks)):
        arrays = after(arrays, packed[-1])
        packed.append(pack_heads(arrays, starts[c], chunks[c]))

    def receive(pieces, gate=None):
        pieces = [pieces[0]] + [swap_planes(pieces[k], k) for k in range(1, PLANES)]
        if gate is not None:
            pieces[1:] = after(pieces[1:], gate)
        low = stack(pieces[:2])
        chip_low = swap(low, 2)
        if gate is None:
            pieces[2:] = after(pieces[2:], chip_low, weight_sides, far_rows)
        high = stack(pieces[2:])
        chip_high = swap(high, 2)
        mine = [low, high, swap(low, 1), swap(high, 1)]
        return pieces, mine, [chip_low, chip_high, swap(chip_low, 1), swap(chip_high, 1)]

    received = [receive(packed[0])]

    planes_at = (plane ^ jnp.arange(PLANES, dtype=jnp.int32)) * GROUP
    my_blocks = planes_at + member
    held = jnp.concatenate([planes_at + (member ^ m) for m in range(GROUP)])
    my_pattern = jnp.stack([piece[0, rows, : 2 * REACH] for piece in received[0][0]])
    away = (held[None, :] - my_blocks[:, None]) % blocks
    full = (away == 0).astype(jnp.int32)
    for offset in list(range(-REACH, 0)) + list(range(1, REACH + 1)):
        chosen = (my_pattern[:, column_of(offset)] != 0)[:, None]
        full = full + (chosen & (away == offset % blocks)).astype(jnp.int32)
    is_ref = jnp.any(held[:, None] == owners[None, :], axis=1).astype(jnp.int32)
    flags = full + 2 * is_ref[None, :]
    near_flags, far_flags = flags[:, : 2 * PLANES], flags[:, 2 * PLANES :]

    def project(total, near, at, c):
        return total + jnp.dot(near, weight_sides[at][c], preferred_element_type=F32)

    def hand_back(outs):
        back = [outs[0]] + [swap_planes(outs[k], k) for k in range(1, PLANES)]
        return jnp.concatenate(back, axis=1)

    kept = given = jnp.zeros((rows, out_cols), F32)
    outs = None
    for c in range(len(chunks)):
        own, mine, theirs_now = received[c]
        if c > 0:
            own = after(own, outs)
            near_before = hand_back(outs)
        state = attend(near_flags, own, mine, None, False)
        if c > 0:
            near_before, state = lax.optimization_barrier((near_before, state))
            kept = project(kept, near_before, 0, c - 1)
            given = project(given, near_before, 1, c - 1)
        if c + 1 < len(chunks):
            coming = [packed[c + 1][0]] + list(
                after(tuple(packed[c + 1][1:]), own[1], own[2])
            )
            received.append(receive(coming, state))
            state = after(state, received[-1][1][0])
        outs = attend(far_flags, own, theirs_now, list(state), True)
    near = hand_back(outs)
    far = across(near)
    mixed = project(kept, near, 0, final)
    if final > 0:
        taken = across(given.astype(BF16))
        mixed = mixed + taken.astype(F32)
    far, mixed = lax.optimization_barrier((far, mixed))
    pair_width = far.shape[1] // 2
    pairs = [
        lax.dynamic_slice_in_dim(far, at * pair_width, pair_width, 1) for at in (core, 1 - core)
    ]
    mixed = mixed + jnp.dot(
        jnp.concatenate(pairs, axis=1), far_rows, preferred_element_type=F32
    )
    return mixed.astype(BF16)


def body(query_rows, key_rows, value_rows, pattern, owners, out_weight):
    fits = (
        lax.axis_size("seq") == GROUP * PLANES
        and lax.axis_size("head") == 2
        and (query_rows.shape[1] // HD) % PLANES == 0
    )
    plan = grouped_body if fits else plain_body
    return plan(query_rows, key_rows, value_rows, pattern, owners, out_weight)


def solution(mesh):
    return jax.shard_map(
        body,
        mesh=mesh,
        in_specs=(
            P("seq", "head"),
            P("seq", "head"),
            P("seq", "head"),
            P("seq", None),
            P(),
            P("head", None),
        ),
        out_specs=P("seq", "head"),
        check_vma=False,
    )
```
